512 devices in a mesh: dp: 64 (over x, z), grp: 8 (over y, core).
Axes of the slice: x: 4, y: 4, z: 16, core: 2. Of those that a mesh axis runs over, the one named last changes fastest.
Arguments:
- embeddings: bfloat16 [65536, 768], P(('dp', 'grp')), may hold values from -6 to 6
- cluster: int32 [65536, 1], P(('dp', 'grp')), may hold values from 0 to 63; in each aligned block of 128 rows (0 to 127, 128 to 255, ...) at most 4 rows name the same one
- rank: int32 [65536], P(('dp', 'grp')), may hold values from 0 to 65535, each once
Outputs:
- best_cosine: float32 [65536], P(('dp', 'grp'))
The draws below stay inside these ranges and needn't reach their ends.
Inputs may be any that keep to these rules, and one draw needn't show every extreme that they name: Among the rows of one device, no cluster is named by more than 4 rows, a bound that some block reaches. `rank`: each number appears once.
All inputs are finite; a program needn't handle non-finite values.
Results may differ from the reference program's by a relative error of at most 0.0014.
Values may be sent and summed in bfloat16 or wider, within the bound.
A program may use at most 64 MiB of HBM per device.

```python
import math
import jax
import jax.numpy as jnp
import numpy as np
from jax import lax

D = 768
ROW_DEV = 128
ROWS = 65536
CLUSTERS = 64
MOST = 4
N_DP = 64
N_GRP = 8


def levels(stream_key, dims, cuts, least, high):
    factor_of = 1.0
    for axis_at, parts in cuts:
        steps = jax.random.uniform(jax.random.fold_in(jax.random.fold_in(stream_key, 6), axis_at), (parts,), jnp.float32, least / len(cuts), high / len(cuts))
        factor_of = factor_of * jnp.repeat(jnp.exp(steps), dims[axis_at] // parts).reshape((-1,) + (1,) * (len(dims) - 1 - axis_at))
    return factor_of


def assign_block(own_key, own, number, rows, amount, top, reach, slope):
    order = jax.random.permutation(own_key, amount)
    crowded, usual = shares(amount, rows * top, reach, slope, True), shares(amount, rows * top, reach, slope, False)
    places = jnp.arange(amount)

    def named(lengths, turn):
        used = int((lengths > 0).sum())
        fixed = max(1, used // 4)
        passed = fixed + (places - fixed + turn * (used - fixed)) % max(1, amount - fixed)
        return jnp.zeros((amount,), jnp.int32).at[order[jnp.where(places < fixed, places, passed)]].set(jnp.asarray(lengths, jnp.int32))

    lengths = jnp.where(number % 4 == 0, named(crowded, number // 4), named(usual, number - number // 4 - 1))
    mixed = jax.random.permutation(jax.random.fold_in(own, 3), amount)
    donor, receiver = mixed[0:amount // 2 * 2:2], mixed[1:amount // 2 * 2:2]
    slack = jnp.minimum(lengths[donor] - 1, reach - lengths[receiver]) // 2
    slack = jnp.where((donor == order[0]) | (receiver == order[0]) | (lengths[receiver] == 0), 0, jnp.maximum(slack, 0))
    passed = jax.random.randint(jax.random.fold_in(own, 4), (amount // 2,), 0, 1 << 20) % (slack + 1)
    lengths = lengths.at[donor].add(-passed).at[receiver].add(passed)
    items = jnp.searchsorted(jnp.cumsum(lengths), jnp.arange(rows * top), side="right").astype(jnp.int32)
    table = items.reshape(top, rows).T
    table = table[jax.random.permutation(jax.random.fold_in(own, 1), rows)]
    turn = jax.random.randint(jax.random.fold_in(own, 2), (rows, 1), 0, top)
    return jnp.take_along_axis(table, (jnp.arange(top)[None, :] + turn) % top, axis=1)


def shares(amount, total, most, skew, full):
    portions = [(1 << 20) // math.isqrt(grade ** skew) + 1 for grade in range(1, amount + 1)]
    largest = most if full else min(most, max(-(-total // amount), total * portions[0] // sum(portions)))
    least = 1 if total - largest >= amount - 1 else 0
    given, spare = [largest] + [least] * (amount - 1), total - largest - least * (amount - 1)
    while spare > 0:
        candidates = [i for i in range(1, amount) if given[i] < largest] or [i for i in range(1, amount) if given[i] < most]
        whole, budget = sum([portions[i] for i in candidates]), spare
        for i in candidates:
            more = min(most - given[i], max(1, budget * portions[i] // whole), spare)
            given[i] = given[i] + more
            spare = spare - more
    return np.array(given)


def scatter_about(own_key, shape, width, reach, shards=(), kind=jnp.bfloat16):
    entries = width * jax.random.normal(own_key, shape, jnp.float32)
    if shards:
        entries = entries * levels(own_key, shape, shards, -0.22, 0.18)
    return jnp.clip(entries, -reach, reach).astype(kind)


def setup_inputs(seed: int = 0) -> dict:
    streams_of = jax.random.split(jax.random.key(seed), 4)
    embeddings = scatter_about(streams_of[0], (ROWS, D), 1.0, 6.0, ((0, 512),))
    cluster_keys = jax.random.split(jax.random.fold_in(streams_of[1], 1), ROWS // ROW_DEV)
    cluster_turns = jax.random.permutation(jax.random.fold_in(streams_of[1], 3), ROWS // ROW_DEV)
    cluster = jax.vmap(lambda own, number: assign_block(jax.random.fold_in(streams_of[1], 2), own, number, ROW_DEV, CLUSTERS, 1, MOST, 2))(cluster_keys, cluster_turns).reshape((ROWS, 1))
    rank = jax.random.permutation(streams_of[2], ROWS).astype(jnp.int32)
    return dict(embeddings=embeddings, cluster=cluster, rank=rank)


def reference(embeddings, cluster, rank):
    labels = cluster[:, 0]
    values = embeddings.astype(jnp.float32)
    scale = lax.rsqrt(lax.optimization_barrier(jnp.mean(values * values, axis=1, keepdims=True)) + 1e-06) / jnp.sqrt(jnp.float32(D))
    unit = (values * scale).astype(jnp.bfloat16)
    capacity = N_GRP * N_DP * MOST
    order = jnp.argsort(labels, stable=True).astype(jnp.int32)
    counts = lax.optimization_barrier(jnp.sum((labels[:, None] == jnp.arange(CLUSTERS, dtype=jnp.int32)[None, :]).astype(jnp.int32), axis=0))
    starts = (jnp.cumsum(counts) - counts).astype(jnp.int32)
    padded_order = jnp.concatenate([order, jnp.full((capacity,), ROWS, jnp.int32)])
    unit_pad = jnp.concatenate([unit, jnp.zeros((1, D), jnp.bfloat16)], axis=0)
    rank_pad = jnp.concatenate([rank, jnp.full((1,), 2 ** 30, jnp.int32)])

    def one_cluster(index):
        members = lax.dynamic_slice_in_dim(padded_order, starts[index], capacity)
        live = jnp.arange(capacity, dtype=jnp.int32) < counts[index]
        members = jnp.where(live, members, ROWS).astype(jnp.int32)
        rows = unit_pad[members]
        ranks = rank_pad[members]
        cosine = jnp.dot(rows, rows.T, preferred_element_type=jnp.float32)
        masked = jnp.where(ranks[None, :] < ranks[:, None], cosine, -jnp.inf)
        best = jnp.maximum(lax.optimization_barrier(jnp.max(masked, axis=1)), -1.0)
        return (members, best)
    members, best = lax.map(one_cluster, jnp.arange(CLUSTERS, dtype=jnp.int32))
    result = jnp.zeros((ROWS + 1,), jnp.float32).at[members.reshape(-1)].set(best.reshape(-1))
    return result[:ROWS]
```

```python
import jax
import jax.numpy as jnp
from jax import lax
from jax.experimental import pallas as pl
from jax.experimental.pallas import tpu as pltpu
from jax.sharding import PartitionSpec as P

NX, NY, NZ = 4, 4, 16
MOST = 4
CHUNKS = 4
PER = NZ // CHUNKS
ROWS = NX * MOST
SLOTS = NZ * ROWS
EMPTY = 65536.0

OFF = [0]
for step in range(1, NZ // 2 + 1):
    OFF += [step, -step]
OFF = OFF[:NZ]

F32, BF16 = jnp.float32, jnp.bfloat16


def iota(shape, dim):
    return lax.broadcasted_iota(jnp.int32, shape, dim)


def onehot(cond):
    return jnp.where(cond, 1.0, 0.0)


def dot(a, b):
    return lax.dot_general(a, b, (((1,), (0,)), ((), ())), preferred_element_type=F32)


def kernel(emb, lab, rank, out, S, Sr, R1, Rr1, Rr2, T, K, Q2, KR, QR2, PM, PMs, BS, B0, B1, V,
           z_s, z_r, zr_s, zr_r, x_s, x_r, xr_s, xr_r, y_s, y_r, yr_s, yr_r, pm_s, pm_r, b_s, b_r, v_s, v_r):
    dp, grp = lax.axis_index("dp"), lax.axis_index("grp")
    x, z = lax.div(dp, NZ), lax.rem(dp, NZ)
    y, core = lax.div(grp, 2), lax.rem(grp, 2)
    z_at = [lax.rem(z + off + NZ, NZ) for off in OFF]
    z_from = [lax.rem(z - off + NZ, NZ) for off in OFF]
    x_at = [lax.rem(x + q, NX) for q in range(NX)]
    x_from = [lax.rem(x - q + NX, NX) for q in range(NX)]
    y_at = [lax.rem(y + q, NY) for q in range(NY)]

    def along_z(zz):
        return (x * NZ + zz, grp)

    def along_x(xx):
        return (xx * NZ + z, grp)

    def along_y(yy):
        return (dp, yy * 2 + core)

    sibling = (dp, y * 2 + 1 - core)
    mesh_id = pl.DeviceIdType.MESH
    started = []

    def send(src, dst, send_sem, recv_sem, to):
        copy = pltpu.make_async_remote_copy(
            src_ref=src, dst_ref=dst, send_sem=send_sem, recv_sem=recv_sem, device_id=to, device_id_type=mesh_id
        )
        copy.start()
        started.append(copy)
        return copy

    barrier = pltpu.get_barrier_semaphore()
    peers = [along_z(z_at[p]) for p in range(1, NZ)] + [along_x(x_at[q]) for q in range(1, NX)]
    peers += [along_y(y_at[q]) for q in range(1, NY)] + [sibling]
    for peer in peers:
        pl.semaphore_signal(barrier, inc=1, device_id=peer, device_id_type=mesh_id)

    lab_row = lab[...].astype(F32)
    i0, i1 = iota((128, 128), 0), iota((128, 128), 1)
    lab_all = jnp.broadcast_to(lab_row, (128, 128))
    lab_col = jnp.sum(jnp.where(i0 == i1, lab_all, 0.0), axis=1, keepdims=True)
    same = onehot(lab_col == lab_all)
    slot_row = jnp.sum(jnp.where(i0 < i1, same, 0.0), axis=0, keepdims=True)
    slot_col = jnp.sum(jnp.where(i1 < i0, same, 0.0), axis=1, keepdims=True)
    xg_row = jnp.floor(lab_row * (1.0 / NZ))
    zg_row = lab_row - NZ * xg_row
    xg_col = jnp.floor(lab_col * (1.0 / NZ))
    pos_row = zg_row * ROWS + xg_row * MOST + slot_row

    rank_row = rank[...].astype(F32)
    high = jnp.floor(rank_row * (1.0 / 256))
    low = rank_row - 256.0 * high
    mine = zg_row == iota((NZ, 128), 0).astype(F32)
    parts = jnp.concatenate(
        [jnp.where(mine, high, 0.0), jnp.where(mine, low, 0.0), onehot(mine)], axis=0
    ).astype(BF16)
    place = onehot(xg_col * MOST + slot_col == i1.astype(F32)).astype(BF16)
    found = dot(parts, place)
    ranks = found[:NZ] * 256.0 + found[NZ:2 * NZ] + (1.0 - found[2 * NZ:]) * EMPTY
    for i in range(NZ):
        Sr[i] = ranks[i:i + 1]

    values = emb[...].astype(F32)
    scale = lax.rsqrt(jnp.mean(values * values, axis=1, keepdims=True) + 1e-06) / jnp.sqrt(F32(values.shape[1]))
    unit = (values * scale).astype(BF16)
    spread = onehot(pos_row == iota((SLOTS, 128), 0).astype(F32)).astype(BF16)
    slots = dot(spread, unit).astype(BF16)
    for i in range(NZ):
        S[i] = slots[i * ROWS:(i + 1) * ROWS]

    pl.semaphore_wait(barrier, len(peers))

    z_copy, zr_copy = [None], [None]
    for p in range(1, NZ):
        zr_copy.append(send(Sr.at[z_at[p]], Rr1.at[p], zr_s.at[p], zr_r.at[p], along_z(z_at[p])))
    for p in range(1, NZ):
        z_copy.append(send(S.at[z_at[p]], R1.at[p], z_s.at[p], z_r.at[p], along_z(z_at[p])))
    Rr1[0] = Sr[z]
    R1[0] = S[z]

    for p in range(1, NZ):
        zr_copy[p].wait_recv()
    xr_copy = [None]
    for q in range(1, NX):
        xr_copy.append(send(Rr1, Rr2.at[q], xr_s.at[q], xr_r.at[q], along_x(x_at[q])))
    Rr2[0] = Rr1[...]
    for q in range(1, NX):
        xr_copy[q].wait_recv()
    lanes = Rr2[...].reshape(NX * NZ, 128)
    lane_high = jnp.floor(lanes * (1.0 / 256))
    lane_low = lanes - 256.0 * lane_high
    r0, r1 = iota((SLOTS, NX * NZ), 0), iota((SLOTS, NX * NZ), 1)
    chunk_of, q_of, place_of = r0 // (ROWS * PER), (r0 // ROWS) % NX, (r0 // MOST) % PER
    pick = onehot(r1 == q_of * NZ + chunk_of * PER + place_of).astype(BF16)
    both = dot(pick, jnp.concatenate([lane_high, lane_low], axis=1).astype(BF16))
    wide = both[:, :128] * 256.0 + both[:, 128:]
    w0, w1 = iota((SLOTS, 128), 0), iota((SLOTS, 128), 1)
    own_col = jnp.sum(jnp.where(w1 == x * MOST + w0 % MOST, wide, 0.0), axis=1, keepdims=True)
    d0, d1 = iota((SLOTS, SLOTS), 0), iota((SLOTS, SLOTS), 1)
    KR[0] = jnp.sum(jnp.where(d0 == d1, own_col, 0.0), axis=0, keepdims=True)
    yr_copy = [None]
    for q in range(1, NY):
        yr_copy.append(send(KR.at[0], KR.at[NY - q], yr_s.at[q], yr_r.at[q], along_y(y_at[q])))
    qr_copy = send(KR.at[0], QR2, yr_s.at[0], yr_r.at[0], sibling)

    o0, o1 = iota((PER * ROWS, PER * ROWS), 0), iota((PER * ROWS, PER * ROWS), 1)
    from_x = lax.rem(x + o0 // ROWS, NX)
    order = onehot(o1 == ((o0 // MOST) % PER) * ROWS + from_x * MOST + o0 % MOST).astype(BF16)
    up, down = along_y(y_at[1]), along_y(y_at[NY - 1])
    for t in range(CHUNKS):
        for p in range(t * PER, (t + 1) * PER):
            if p:
                z_copy[p].wait_recv()
        rows = R1[t * PER:(t + 1) * PER].reshape(PER * ROWS, R1.shape[2])
        turned = dot(order, rows).astype(BF16)
        x_copy = []
        for q in range(1, NX):
            T[t, q] = turned[q * ROWS:(q + 1) * ROWS]
            x_copy.append(send(T.at[t, q], K.at[0, t, q], x_s.at[t, q], x_r.at[t, q], along_x(x_at[q])))
        K[0, t, 0] = turned[:ROWS]
        for copy in x_copy:
            copy.wait_recv()
        to_up = send(K.at[0, t], K.at[NY - 1, t], y_s.at[t, 0], y_r.at[t, 0], up)
        to_down = send(K.at[0, t], K.at[1, t], y_s.at[t, 1], y_r.at[t, 1], down)
        q2_copy = send(K.at[0, t], Q2.at[t], y_s.at[t, 2], y_r.at[t, 2], sibling)
        to_up.wait_recv()
        on_up = send(K.at[NY - 1, t, pl.ds(0, 2)], K.at[2, t, pl.ds(0, 2)], y_s.at[t, 3], y_r.at[t, 3], up)
        to_down.wait_recv()
        on_down = send(K.at[1, t, pl.ds(2, 2)], K.at[2, t, pl.ds(2, 2)], y_s.at[t, 4], y_r.at[t, 4], down)
        q2_copy.wait_recv()
        on_up.wait_recv()
        on_down.wait_recv()

    for q in range(1, NY):
        yr_copy[q].wait_recv()
    qr_copy.wait_recv()

    width = K.shape[4]
    query_rank = jnp.concatenate([KR[0], QR2[...]], axis=1)
    best = None
    for b in range(NY):
        key_rank = jnp.sum(jnp.where(d0 == d1, KR[b], 0.0), axis=1, keepdims=True)
        keys = K[b].reshape(SLOTS, width)
        halves = []
        for queries, ranks_q in ((K[0], query_rank[:, :SLOTS]), (Q2[...], query_rank[:, SLOTS:])):
            cosine = lax.dot_general(
                keys, queries.reshape(SLOTS, width), (((1,), (1,)), ((), ())), preferred_element_type=F32
            )
            masked = jnp.where(key_rank < ranks_q, cosine, -jnp.inf)
            halves.append(jnp.max(masked, axis=0, keepdims=True))
        best = halves if best is None else [jnp.maximum(a, b_) for a, b_ in zip(best, halves)]
    PMs[...] = best[1]
    pm_copy = send(PMs, PM, pm_s, pm_r, sibling)
    pm_copy.wait_recv()
    result = jnp.maximum(jnp.maximum(best[0], PM[...]), -1.0)

    BS[0:1] = result[:, :128]
    BS[1:2] = result[:, 128:]
    b_copy = []
    for q in range(1, NX):
        b_copy.append(send(BS, B0.at[q], b_s.at[q], b_r.at[q], along_x(x_from[q])))
    B0[0] = BS[...]
    for copy in b_copy:
        copy.wait_recv()
    for q in range(NX):
        for h in range(2):
            B1[h, q:q + 1] = B0[q, h:h + 1]
    v_copy = []
    for p in range(1, NZ):
        v_copy.append(send(B1.at[p // 8], V.at[p], v_s.at[p], v_r.at[p], along_z(z_from[p])))
    V[0] = B1[0]
    for copy in v_copy:
        copy.wait_recv()
    back = V[...].reshape(NZ * NX, 128)
    a0, a1 = iota((NZ * NX, 128), 0), iota((NZ * NX, 128), 1)
    p_of, q_at = a0 // NX, a0 % NX
    first = ((p_of // PER) % 2) * (ROWS * PER) + q_at * ROWS + (p_of % PER) * MOST
    held = jnp.where((a1 >= first) & (a1 < first + MOST), back, 0.0)
    shift = 64
    while shift >= MOST:
        held = held + pltpu.roll(held, shift, 1)
        shift //= 2
    off = jnp.where(p_of % 2 == 1, (p_of + 1) // 2, -(p_of // 2))
    cluster_of = (lax.rem(x + q_at, NX) * NZ + lax.rem(z + off + NZ, NZ)).astype(F32)
    chosen = jnp.zeros((NZ * NX, 128), F32)
    for s in range(MOST):
        hit = (cluster_of == lab_row) & (slot_row == float(s))
        chosen = chosen + jnp.where(hit, held[:, s:s + 1], 0.0)
    out[...] = jnp.sum(chosen, axis=0, keepdims=True)

    for copy in started:
        copy.wait_send()


def body(embeddings, cluster, rank):
    width = embeddings.shape[1]
    vmem = pl.BlockSpec(memory_space=pltpu.VMEM)
    sem = pltpu.SemaphoreType.DMA
    out = pl.pallas_call(
        kernel,
        out_shape=jax.ShapeDtypeStruct((1, 128), F32),
        in_specs=[vmem] * 3,
        out_specs=vmem,
        scratch_shapes=[
            pltpu.VMEM((NZ, ROWS, width), BF16),
            pltpu.VMEM((NZ, 1, 128), F32),
            pltpu.VMEM((NZ, ROWS, width), BF16),
            pltpu.VMEM((NZ, 1, 128), F32),
            pltpu.VMEM((NX, NZ, 1, 128), F32),
            pltpu.VMEM((CHUNKS, NX, ROWS, width), BF16),
            pltpu.VMEM((NY, CHUNKS, NX, ROWS, width), BF16),
            pltpu.VMEM((CHUNKS, NX, ROWS, width), BF16),
            pltpu.VMEM((NY, 1, SLOTS), F32),
            pltpu.VMEM((1, SLOTS), F32),
            pltpu.VMEM((1, SLOTS), F32),
            pltpu.VMEM((1, SLOTS), F32),
            pltpu.VMEM((2, 128), F32),
            pltpu.VMEM((NX, 2, 128), F32),
            pltpu.VMEM((2, NX, 128), F32),
            pltpu.VMEM((NZ, NX, 128), F32),
            sem((NZ,)), sem((NZ,)), sem((NZ,)), sem((NZ,)),
            sem((CHUNKS, NX)), sem((CHUNKS, NX)), sem((NX,)), sem((NX,)),
            sem((CHUNKS, 5)), sem((CHUNKS, 5)), sem((NY,)), sem((NY,)),
            sem, sem, sem((NX,)), sem((NX,)), sem((NZ,)), sem((NZ,)),
        ],
        compiler_params=pltpu.CompilerParams(
            collective_id=0, has_side_effects=True, vmem_limit_bytes=40 * 1024 * 1024
        ),
    )(embeddings, cluster.reshape(1, 128), rank.reshape(1, 128))
    return out.reshape(128)


def solution(mesh):
    in_specs = (P(("dp", "grp"), None), P(("dp", "grp"), None), P(("dp", "grp")))
    out_specs = P(("dp", "grp"))
    return jax.shard_map(body, mesh=mesh, in_specs=in_specs, out_specs=out_specs, check_vma=False)
```

```python
import jax
import jax.numpy as jnp
from jax import lax
from jax.experimental import pallas as pl
from jax.experimental.pallas import tpu as pltpu
from jax.sharding import PartitionSpec as P

NX, NY, NZ = 4, 4, 16
GROUPS = NX * NZ
MOST = 4
SLOTS = GROUPS * MOST
CHUNKS = 4
PER = GROUPS // CHUNKS
CHUNK = PER * MOST
EMPTY = 65536.0

DZ = [8 - i // 2 if i % 2 == 0 else (i + 1) // 2 - 8 for i in range(NZ)]
DX = [2, 1, 3, 0]
PLACES = [(dx, dz) for dx in DX for dz in DZ]
LAST = GROUPS - 1

F32, BF16 = jnp.float32, jnp.bfloat16


def iota(shape, dim):
    return lax.broadcasted_iota(jnp.int32, shape, dim)


def onehot(cond):
    return jnp.where(cond, 1.0, 0.0)


def dot(a, b):
    return lax.dot_general(a, b, (((1,), (0,)), ((), ())), preferred_element_type=F32)


def kernel(emb_in, lab_in, rank_in, out, emb, lab, rank, S, Sr, R, Rr, K, Q2, KR, QR2, PM, PMs, BS, V,
           in_s, row_s, row_r, rr_s, rr_r, y_s, y_r, yr_s, yr_r, pm_s, pm_r, b_s, b_r):
    dp, grp = lax.axis_index("dp"), lax.axis_index("grp")
    x, z = lax.div(dp, NZ), lax.rem(dp, NZ)
    y, core = lax.div(grp, 2), lax.rem(grp, 2)
    z_at = {dz: lax.rem(z + (dz + NZ), NZ) for dz in range(1 - NZ // 2, NZ // 2 + 1)}
    z_from = {dz: lax.rem(z + (NZ - dz), NZ) for dz in z_at}
    x_at = [lax.rem(x + dx, NX) * NZ for dx in range(NX)]
    x_from = [lax.rem(x + (NX - dx), NX) * NZ for dx in range(NX)]
    y_at = [lax.rem(y + q, NY) for q in range(NY)]
    target = [x_at[dx] + z_at[dz] for dx, dz in PLACES]
    source = [x_from[dx] + z_from[dz] for dx, dz in PLACES]

    def along_y(q):
        return (dp, y_at[q] * 2 + core)

    sibling = (dp, y * 2 + 1 - core)
    mesh_id = pl.DeviceIdType.MESH
    started = []

    def send(src, dst, send_sem, recv_sem, to, keep=True):
        copy = pltpu.make_async_remote_copy(
            src_ref=src, dst_ref=dst, send_sem=send_sem, recv_sem=recv_sem, device_id=to, device_id_type=mesh_id
        )
        copy.start()
        if keep:
            started.append(copy)
        return copy

    def wait_all(ref, sem):
        pltpu.make_async_copy(ref, ref, sem).wait()

    barrier = pltpu.get_barrier_semaphore()
    peers = [(target[p], grp) for p in range(LAST)] + [along_y(q) for q in range(1, NY)] + [sibling]
    for peer in peers:
        pl.semaphore_signal(barrier, inc=1, device_id=peer, device_id_type=mesh_id)

    loads = [pltpu.make_async_copy(a, b, in_s.at[i]) for i, (a, b) in enumerate(
        ((lab_in, lab), (rank_in, rank), (emb_in, emb)))]
    for load in loads:
        load.start()
    loads[0].wait()
    loads[1].wait()

    lab_row = lab[...].astype(F32)
    i0, i1 = iota((128, 128), 0), iota((128, 128), 1)
    lab_all = jnp.broadcast_to(lab_row, (128, 128))
    lab_col = jnp.sum(jnp.where(i0 == i1, lab_all, 0.0), axis=1, keepdims=True)
    same = onehot(lab_col == lab_all)
    slot_row = jnp.sum(jnp.where(i0 < i1, same, 0.0), axis=0, keepdims=True)
    slot_col = jnp.sum(jnp.where(i1 < i0, same, 0.0), axis=1, keepdims=True)
    pos_row = lab_row * MOST + slot_row
    pos_col = lab_col * MOST + slot_col

    rank_row = rank[...].astype(F32)
    high = jnp.floor(rank_row * (1.0 / 256))
    low = rank_row - 256.0 * high
    half_row = jnp.floor(pos_row * (1.0 / 128))
    half_col = jnp.floor(pos_col * (1.0 / 128))
    mine = half_row == iota((8, 128), 0).astype(F32)
    parts = jnp.concatenate(
        [jnp.where(mine, high, 0.0), jnp.where(mine, low, 0.0), onehot(mine)], axis=0
    ).astype(BF16)
    place = onehot(pos_col - 128.0 * half_col == i1.astype(F32)).astype(BF16)
    found = dot(parts, place)
    ranks = found[:8] * 256.0 + found[8:16] + (1.0 - found[16:]) * EMPTY
    for i in range(2):
        Sr[i] = ranks[i:i + 1]

    width = emb.shape[1]
    half = width // 2
    s0, s1 = iota((2 * SLOTS, 256), 0), iota((2 * SLOTS, 256), 1)
    slot_of = (s0 // 8) * MOST + s0 % MOST
    pos_two = jnp.concatenate([pos_row, pos_row], axis=1)
    spread = onehot((pos_two == slot_of.astype(F32)) & ((s0 // MOST) % 2 == s1 // 128)).astype(BF16)
    loads[2].wait()
    values = emb[...].astype(F32)
    scale = lax.rsqrt(jnp.mean(values * values, axis=1, keepdims=True) + 1e-06) / jnp.sqrt(F32(width))
    unit = (values * scale).astype(BF16)
    S[...] = dot(spread, jnp.concatenate([unit[:, :half], unit[:, half:]], axis=0)).astype(BF16).reshape(S.shape)

    pl.semaphore_wait(barrier, len(peers))

    def send_rows(places):
        for p in places:
            send(S.at[target[p]], R.at[p], row_s, row_r.at[p // PER], (target[p], grp), False)

    send_rows(range(PER))
    for p in range(LAST):
        send(Sr.at[lax.div(target[p], 32)], Rr.at[p], rr_s, rr_r, (target[p], grp), False)
    send_rows(range(PER, LAST))
    R[LAST] = S[dp]
    Rr[LAST] = Sr[lax.div(dp, 32)]

    o0, o1 = iota((2 * CHUNK, 2 * CHUNK), 0), iota((2 * CHUNK, 2 * CHUNK), 1)
    whole = onehot(o1 == ((o0 % CHUNK) // MOST) * 8 + (o0 // CHUNK) * MOST + o0 % MOST).astype(BF16)
    up, down = along_y(1), along_y(NY - 1)
    from_down, from_up, q2_copy, on = {}, {}, {}, []

    def arrive(t):
        wait_all(R.at[pl.ds(t * PER, PER - (t == CHUNKS - 1))], row_r.at[t])
        rows = dot(whole, R[t * PER:(t + 1) * PER].reshape(2 * CHUNK, half)).astype(BF16)
        K[0, t, :, :half] = rows[:CHUNK]
        K[0, t, :, half:] = rows[CHUNK:]
        from_down[t] = send(K.at[0, t], K.at[NY - 1, t], y_s.at[t, 0], y_r.at[t, 0], up)
        from_up[t] = send(K.at[0, t], K.at[1, t], y_s.at[t, 1], y_r.at[t, 1], down)
        q2_copy[t] = send(K.at[0, t], Q2.at[t], y_s.at[t, 2], y_r.at[t, 2], sibling)

    def forward(t):
        a, b = pl.ds(0, CHUNK // 2), pl.ds(CHUNK // 2, CHUNK // 2)
        from_down[t].wait_recv()
        on.append(send(K.at[NY - 1, t, a], K.at[2, t, a], y_s.at[t, 3], y_r.at[t, 3], up))
        from_up[t].wait_recv()
        on.append(send(K.at[1, t, b], K.at[2, t, b], y_s.at[t, 4], y_r.at[t, 4], down))

    arrive(0)

    wait_all(Rr.at[pl.ds(0, LAST)], rr_r)
    lanes = Rr[...].reshape(GROUPS, 128)
    lane_high = jnp.floor(lanes * (1.0 / 256))
    lane_low = lanes - 256.0 * lane_high
    pick = onehot(iota((SLOTS, GROUPS), 1) == iota((SLOTS, GROUPS), 0) // MOST).astype(BF16)
    both = dot(pick, jnp.concatenate([lane_high, lane_low], axis=1).astype(BF16))
    wide = both[:, :128] * 256.0 + both[:, 128:]
    w0, w1 = iota((SLOTS, 128), 0), iota((SLOTS, 128), 1)
    own_col = jnp.sum(jnp.where(w1 == lax.rem(dp, 32) * MOST + w0 % MOST, wide, 0.0), axis=1, keepdims=True)
    d0, d1 = iota((SLOTS, SLOTS), 0), iota((SLOTS, SLOTS), 1)
    KR[0] = jnp.sum(jnp.where(d0 == d1, own_col, 0.0), axis=0, keepdims=True)
    yr_copy = [send(KR.at[0], KR.at[NY - q], yr_s.at[q], yr_r.at[q], along_y(q)) for q in range(1, NY)]
    yr_copy.append(send(KR.at[0], QR2, yr_s.at[0], yr_r.at[0], sibling))

    arrive(1)
    forward(0)
    arrive(2)
    forward(1)
    arrive(3)
    forward(2)
    forward(3)
    for copy in yr_copy + list(q2_copy.values()) + on:
        copy.wait_recv()

    query_rank = jnp.concatenate([KR[0], QR2[...]], axis=1)
    best = None
    for b in range(NY):
        key_rank = jnp.sum(jnp.where(d0 == d1, KR[b], 0.0), axis=1, keepdims=True)
        keys = K[b].reshape(SLOTS, width)
        halves = []
        for queries, ranks_q in ((K[0], query_rank[:, :SLOTS]), (Q2[...], query_rank[:, SLOTS:])):
            cosine = lax.dot_general(
                keys, queries.reshape(SLOTS, width), (((1,), (1,)), ((), ())), preferred_element_type=F32
            )
            masked = jnp.where(key_rank < ranks_q, cosine, -jnp.inf)
            halves.append(jnp.max(masked, axis=0, keepdims=True))
        best = halves if best is None else [jnp.maximum(a, b_) for a, b_ in zip(best, halves)]
    PMs[...] = best[1]
    send(PMs, PM, pm_s, pm_r, sibling).wait_recv()
    result = jnp.maximum(jnp.maximum(best[0], PM[...]), -1.0)

    BS[0] = result[:, :128]
    BS[1] = result[:, 128:]
    for p in range(LAST):
        send(BS.at[p // 32], V.at[p], b_s, b_r, (source[p], grp), False)
    V[LAST] = BS[1]
    a0, a1 = iota((GROUPS, 128), 0), iota((GROUPS, 128), 1)
    i, j = a0 % NZ, a0 // NZ
    dz = jnp.where(i % 2 == 1, (i + 1) // 2 - 8, 8 - i // 2)
    dx = jnp.where(j == 0, 2, jnp.where(j == 2, 3, 1 - j // 3))
    cluster_of = (lax.rem(x + dx, NX) * NZ + lax.rem(z + dz + NZ, NZ)).astype(F32)
    first = (a0 % 32) * MOST
    wait_all(V.at[pl.ds(0, LAST)], b_r)
    held = jnp.where((a1 >= first) & (a1 < first + MOST), V[...].reshape(GROUPS, 128), 0.0)
    shift = 64
    while shift >= MOST:
        held = held + pltpu.roll(held, shift, 1)
        shift //= 2
    chosen = jnp.zeros((GROUPS, 128), F32)
    for s in range(MOST):
        hit = (cluster_of == lab_row) & (slot_row == float(s))
        chosen = chosen + jnp.where(hit, held[:, s:s + 1], 0.0)
    out[...] = jnp.sum(chosen, axis=0, keepdims=True)

    wait_all(R.at[pl.ds(0, LAST)], row_s)
    wait_all(Rr.at[pl.ds(0, LAST)], rr_s)
    wait_all(V.at[pl.ds(0, LAST)], b_s)
    for copy in started:
        copy.wait_send()


def body(embeddings, cluster, rank):
    rows, width = embeddings.shape
    sem = pltpu.SemaphoreType.DMA
    out = pl.pallas_call(
        kernel,
        out_shape=jax.ShapeDtypeStruct((1, rows), F32),
        in_specs=[pl.BlockSpec(memory_space=pl.ANY)] * 3,
        out_specs=pl.BlockSpec(memory_space=pltpu.VMEM),
        scratch_shapes=[
            pltpu.VMEM((rows, width), BF16),
            pltpu.VMEM((1, rows), jnp.int32),
            pltpu.VMEM((1, rows), jnp.int32),
            pltpu.VMEM((GROUPS, 8, width // 2), BF16),
            pltpu.VMEM((2, 1, 128), F32),
            pltpu.VMEM((GROUPS, 8, width // 2), BF16),
            pltpu.VMEM((GROUPS, 1, 128), F32),
            pltpu.VMEM((NY, CHUNKS, CHUNK, width), BF16),
            pltpu.VMEM((CHUNKS, CHUNK, width), BF16),
            pltpu.VMEM((NY, 1, SLOTS), F32),
            pltpu.VMEM((1, SLOTS), F32),
            pltpu.VMEM((1, SLOTS), F32),
            pltpu.VMEM((1, SLOTS), F32),
            pltpu.VMEM((2, 1, 128), F32),
            pltpu.VMEM((GROUPS, 1, 128), F32),
            sem((3,)),
            sem, sem((CHUNKS,)), sem, sem,
            sem((CHUNKS, 5)), sem((CHUNKS, 5)), sem((NY,)), sem((NY,)),
            sem, sem, sem, sem,
        ],
        compiler_params=pltpu.CompilerParams(
            collective_id=0, has_side_effects=True, vmem_limit_bytes=40 * 1024 * 1024
        ),
    )(embeddings, cluster.reshape(1, rows), rank.reshape(1, rows))
    return out.reshape(rows)


def solution(mesh):
    in_specs = (P(("dp", "grp"), None), P(("dp", "grp"), None), P(("dp", "grp")))
    out_specs = P(("dp", "grp"))
    return jax.shard_map(body, mesh=mesh, in_specs=in_specs, out_specs=out_specs, check_vma=False)
```

```python
import jax
import jax.numpy as jnp
from jax import lax
from jax.experimental import pallas as pl
from jax.experimental.pallas import tpu as pltpu
from jax.sharding import PartitionSpec as P

NX, NY, NZ = 4, 4, 16
GROUPS = NX * NZ
MOST = 4
SLOTS = GROUPS * MOST
EMPTY = 65536.0

REACH = 4
NEAR = [(dx, dz) for dx in (2, 1, 3, 0) for d in range(REACH, 0, -1) for dz in (d, -d)]
NEAR = [place for dx in (2, 1, 3, 0) for place in [n for n in NEAR if n[0] == dx] + [(dx, 0)]]
FAR = [(dx, dz) for dx in (2, 1, 3, 0) for dz in (8, -7, 7, -6, 6, -5, 5)]
FIRST = 28
PLACES = NEAR[:FIRST] + FAR + NEAR[FIRST:]
SPANS = [(0, 16), (16, 28), (28, 44), (44, 56), (56, 64)]
CHUNKS = len(SPANS)
RELAYED = 3
EARLY = SPANS[RELAYED][0] * MOST
LAST = GROUPS - 1

F32, BF16 = jnp.float32, jnp.bfloat16


def iota(shape, dim):
    return lax.broadcasted_iota(jnp.int32, shape, dim)


def onehot(cond):
    return jnp.where(cond, 1.0, 0.0)


def dot(a, b):
    return lax.dot_general(a, b, (((1,), (0,)), ((), ())), preferred_element_type=F32)


def kernel(emb_in, lab_in, rank_in, out, emb, lab, rank, S, Sr, R, Rr, K, Q2, KR, QR2, PM, PMs, BS, V,
           gate, in_s, row_s, row_r, rr_s, rr_r, y_s, y_r, yr_s, yr_r, pm_s, pm_r, b_s, b_r):
    dp, grp = lax.axis_index("dp"), lax.axis_index("grp")
    x, z = lax.div(dp, NZ), lax.rem(dp, NZ)
    y, core = lax.div(grp, 2), lax.rem(grp, 2)
    z_at = {dz: lax.rem(z + (dz + NZ), NZ) for dz in range(1 - NZ // 2, NZ // 2 + 1)}
    z_from = {dz: lax.rem(z + (NZ - dz), NZ) for dz in z_at}
    x_at = [lax.rem(x + dx, NX) * NZ for dx in range(NX)]
    x_from = [lax.rem(x + (NX - dx), NX) * NZ for dx in range(NX)]
    y_at = [lax.rem(y + q, NY) for q in range(NY)]
    target = [x_at[dx] + z_at[dz] for dx, dz in PLACES]
    source = [x_from[dx] + z_from[dz] for dx, dz in PLACES]

    def along_y(q):
        return (dp, y_at[q] * 2 + core)

    sibling = (dp, y * 2 + 1 - core)
    mesh_id = pl.DeviceIdType.MESH
    started = []

    def send(src, dst, send_sem, recv_sem, to, keep=True):
        copy = pltpu.make_async_remote_copy(
            src_ref=src, dst_ref=dst, send_sem=send_sem, recv_sem=recv_sem, device_id=to, device_id_type=mesh_id
        )
        copy.start()
        if keep:
            started.append(copy)
        return copy

    def wait_all(ref, sem):
        pltpu.make_async_copy(ref, ref, sem).wait()

    barrier = pltpu.get_barrier_semaphore()
    far = [abs(dz) > REACH for _, dz in PLACES]
    peers = [(target[p], y * 2 + int(far[p])) for p in range(LAST)] + [along_y(q) for q in range(1, NY)] + [sibling]
    for peer in peers:
        pl.semaphore_signal(barrier, inc=1, device_id=peer, device_id_type=mesh_id)

    def listen(reach, count):
        @pl.when(core == reach)
        def _():
            pl.semaphore_wait(barrier, 2 * count + NY)
            pl.semaphore_signal(gate, inc=1, device_id=sibling, device_id_type=mesh_id)

        @pl.when(core != reach)
        def _():
            pl.semaphore_wait(gate, 1)

    loads = [pltpu.make_async_copy(a, b, in_s.at[i]) for i, (a, b) in enumerate(
        ((lab_in, lab), (rank_in, rank), (emb_in, emb)))]
    for load in loads:
        load.start()
    loads[0].wait()
    loads[1].wait()

    lab_row = lab[...].astype(F32)
    i0, i1 = iota((128, 128), 0), iota((128, 128), 1)
    lab_all = jnp.broadcast_to(lab_row, (128, 128))
    lab_col = jnp.sum(jnp.where(i0 == i1, lab_all, 0.0), axis=1, keepdims=True)
    same = onehot(lab_col == lab_all)
    slot_row = jnp.sum(jnp.where(i0 < i1, same, 0.0), axis=0, keepdims=True)
    slot_col = jnp.sum(jnp.where(i1 < i0, same, 0.0), axis=1, keepdims=True)
    pos_row = lab_row * MOST + slot_row
    pos_col = lab_col * MOST + slot_col

    rank_row = rank[...].astype(F32)
    high = jnp.floor(rank_row * (1.0 / 256))
    low = rank_row - 256.0 * high
    half_row = jnp.floor(pos_row * (1.0 / 128))
    half_col = jnp.floor(pos_col * (1.0 / 128))
    mine = half_row == iota((8, 128), 0).astype(F32)
    parts = jnp.concatenate(
        [jnp.where(mine, high, 0.0), jnp.where(mine, low, 0.0), onehot(mine)], axis=0
    ).astype(BF16)
    place = onehot(pos_col - 128.0 * half_col == i1.astype(F32)).astype(BF16)
    found = dot(parts, place)
    ranks = found[:8] * 256.0 + found[8:16] + (1.0 - found[16:]) * EMPTY
    for i in range(2):
        Sr[i] = ranks[i:i + 1]

    width = emb.shape[1]
    half = width // 2
    s0, s1 = iota((2 * SLOTS, 256), 0), iota((2 * SLOTS, 256), 1)
    slot_of = (s0 // 8) * MOST + s0 % MOST
    pos_two = jnp.concatenate([pos_row, pos_row], axis=1)
    spread = onehot((pos_two == slot_of.astype(F32)) & ((s0 // MOST) % 2 == s1 // 128)).astype(BF16)
    loads[2].wait()
    values = emb[...].astype(F32)
    scale = lax.rsqrt(jnp.mean(values * values, axis=1, keepdims=True) + 1e-06) / jnp.sqrt(F32(width))
    unit = (values * scale).astype(BF16)
    S[...] = dot(spread, jnp.concatenate([unit[:, :half], unit[:, half:]], axis=0)).astype(BF16).reshape(S.shape)

    chunk_of = [t for t, (lo, hi) in enumerate(SPANS) for _ in range(lo, hi)]

    def send_rows(places):
        for p in places:
            send(S.at[target[p]], R.at[p], row_s, row_r.at[chunk_of[p]], (target[p], grp), False)

    def send_ranks(places):
        for p in places:
            send(Sr.at[lax.div(target[p], 32)], Rr.at[p], rr_s, rr_r, (target[p], grp), False)

    listen(0, LAST - sum(far))
    send_rows(range(FIRST))
    send_ranks([p for p in range(LAST) if not far[p]])
    listen(1, sum(far))
    send_ranks([p for p in range(LAST) if far[p]])
    send_rows(range(FIRST, LAST))
    R[LAST] = S[dp]
    Rr[LAST] = Sr[lax.div(dp, 32)]

    up, across, down = along_y(1), along_y(2), along_y(NY - 1)
    from_down, from_up, rest = {}, {}, {t: [] for t in range(CHUNKS)}

    def span(t):
        lo, hi = SPANS[t]
        return lo, hi - lo, pl.ds(lo * MOST, (hi - lo) * MOST)

    def arrive(t):
        lo, places, at = span(t)
        wait_all(R.at[pl.ds(lo, places - (t == CHUNKS - 1))], row_r.at[t])
        count = places * MOST
        o0, o1 = iota((2 * count, 2 * count), 0), iota((2 * count, 2 * count), 1)
        whole = onehot(o1 == ((o0 % count) // MOST) * 8 + (o0 // count) * MOST + o0 % MOST).astype(BF16)
        rows = dot(whole, R[lo:lo + places].reshape(2 * count, half)).astype(BF16)
        K[0, lo * MOST:lo * MOST + count, :half] = rows[:count]
        K[0, lo * MOST:lo * MOST + count, half:] = rows[count:]
        from_down[t] = send(K.at[0, at], K.at[3, at], y_s.at[t, 0], y_r.at[t, 0], up)
        from_up[t] = send(K.at[0, at], K.at[1, at], y_s.at[t, 1], y_r.at[t, 1], down)
        rest[t].append(send(K.at[0, at], Q2.at[at], y_s.at[t, 2], y_r.at[t, 2], sibling))
        if t >= RELAYED:
            rest[t].append(send(K.at[0, at], K.at[2, at], y_s.at[t, 3], y_r.at[t, 3], across))
            rest[t] += [from_down[t], from_up[t]]

    def forward(t):
        lo, places, _ = span(t)
        some = places // 8 * 16
        a, b = pl.ds(lo * MOST, some), pl.ds(lo * MOST + some, places * MOST - some)
        from_down[t].wait_recv()
        rest[t].append(send(K.at[3, a], K.at[2, a], y_s.at[t, 3], y_r.at[t, 3], up))
        from_up[t].wait_recv()
        rest[t].append(send(K.at[1, b], K.at[2, b], y_s.at[t, 4], y_r.at[t, 4], down))

    arrive(0)
    arrive(1)
    forward(0)
    arrive(2)
    forward(1)

    wait_all(Rr.at[pl.ds(0, LAST)], rr_r)
    lanes = Rr[...].reshape(GROUPS, 128)
    lane_high = jnp.floor(lanes * (1.0 / 256))
    lane_low = lanes - 256.0 * lane_high
    pick = onehot(iota((SLOTS, GROUPS), 1) == iota((SLOTS, GROUPS), 0) // MOST).astype(BF16)
    both = dot(pick, jnp.concatenate([lane_high, lane_low], axis=1).astype(BF16))
    wide = both[:, :128] * 256.0 + both[:, 128:]
    w0, w1 = iota((SLOTS, 128), 0), iota((SLOTS, 128), 1)
    own_col = jnp.sum(jnp.where(w1 == lax.rem(dp, 32) * MOST + w0 % MOST, wide, 0.0), axis=1, keepdims=True)
    d0, d1 = iota((SLOTS, SLOTS), 0), iota((SLOTS, SLOTS), 1)
    KR[0] = jnp.sum(jnp.where(d0 == d1, own_col, 0.0), axis=0, keepdims=True)
    yr_copy = [send(KR.at[0], KR.at[NY - q], yr_s.at[q], yr_r.at[q], along_y(q)) for q in range(1, NY)]
    yr_copy.append(send(KR.at[0], QR2, yr_s.at[0], yr_r.at[0], sibling))

    arrive(3)
    forward(2)
    arrive(4)

    rows8 = iota((8, 128), 0)
    cluster_of = []
    for p in range(0, GROUPS, 8):
        block = jnp.zeros((8, 128), jnp.int32)
        for i in range(8):
            block = jnp.where(rows8 == i, target[p + i] if p + i < LAST else dp, block)
        cluster_of.append(block)
    cluster_of = jnp.concatenate(cluster_of, axis=0).astype(F32)

    def cosines(best, keys, key_rank, queries, ranks_q):
        cosine = lax.dot_general(keys, queries, (((1,), (1,)), ((), ())), preferred_element_type=F32)
        masked = jnp.where(key_rank < ranks_q, cosine, -jnp.inf)
        return jnp.maximum(best, jnp.max(masked, axis=0, keepdims=True))

    for copy in yr_copy:
        copy.wait_recv()
    query_rank = [KR[0], QR2[...]]
    key_rank = [jnp.sum(jnp.where(d0 == d1, KR[b], 0.0), axis=1, keepdims=True) for b in range(NY)]
    for t in range(RELAYED):
        for copy in rest[t]:
            copy.wait_recv()
    early = [jnp.full((1, EARLY), -1.0, F32)] * 2
    for b in range(NY):
        for c, queries in enumerate((K[0, :EARLY], Q2[:EARLY])):
            early[c] = cosines(early[c], K[b, :EARLY], key_rank[b][:EARLY], queries, query_rank[c][:, :EARLY])
    for t in range(RELAYED, CHUNKS):
        for copy in rest[t]:
            copy.wait_recv()
    late = [jnp.full((1, SLOTS - EARLY), -1.0, F32)] * 2
    best = [jnp.full((1, SLOTS), -1.0, F32)] * 2
    for b in range(NY):
        for c, queries in enumerate((K.at[0], Q2)):
            late[c] = cosines(late[c], K[b, :EARLY], key_rank[b][:EARLY], queries[EARLY:], query_rank[c][:, EARLY:])
            best[c] = cosines(best[c], K[b, EARLY:], key_rank[b][EARLY:], queries[...], query_rank[c])
    best = [jnp.maximum(best[c], jnp.concatenate([early[c], late[c]], axis=1)) for c in range(2)]
    PMs[...] = best[1]
    send(PMs, PM, pm_s, pm_r, sibling).wait_recv()
    result = jnp.maximum(best[0], PM[...])

    BS[0] = result[:, :128]
    BS[1] = result[:, 128:]
    hops = [min(dx, NX - dx) + abs(dz) for dx, dz in PLACES]
    for p in sorted(range(LAST), key=lambda p: -hops[p]):
        send(BS.at[p // 32], V.at[p], b_s, b_r, (source[p], grp), False)
    V[LAST] = BS[1]
    a0, a1 = iota((GROUPS, 128), 0), iota((GROUPS, 128), 1)
    first = (a0 % 32) * MOST
    wait_all(V.at[pl.ds(0, LAST)], b_r)
    held = jnp.where((a1 >= first) & (a1 < first + MOST), V[...].reshape(GROUPS, 128), 0.0)
    shift = 64
    while shift >= MOST:
        held = held + pltpu.roll(held, shift, 1)
        shift //= 2
    chosen = jnp.zeros((GROUPS, 128), F32)
    for s in range(MOST):
        hit = (cluster_of == lab_row) & (slot_row == float(s))
        chosen = chosen + jnp.where(hit, held[:, s:s + 1], 0.0)
    out[...] = jnp.sum(chosen, axis=0, keepdims=True)

    wait_all(R.at[pl.ds(0, LAST)], row_s)
    wait_all(Rr.at[pl.ds(0, LAST)], rr_s)
    wait_all(V.at[pl.ds(0, LAST)], b_s)
    for copy in started:
        copy.wait_send()


def body(embeddings, cluster, rank):
    rows, width = embeddings.shape
    sem = pltpu.SemaphoreType.DMA
    out = pl.pallas_call(
        kernel,
        out_shape=jax.ShapeDtypeStruct((1, rows), F32),
        in_specs=[pl.BlockSpec(memory_space=pl.ANY)] * 3,
        out_specs=pl.BlockSpec(memory_space=pltpu.VMEM),
        scratch_shapes=[
            pltpu.VMEM((rows, width), BF16),
            pltpu.VMEM((1, rows), jnp.int32),
            pltpu.VMEM((1, rows), jnp.int32),
            pltpu.VMEM((GROUPS, 8, width // 2), BF16),
            pltpu.VMEM((2, 1, 128), F32),
            pltpu.VMEM((GROUPS, 8, width // 2), BF16),
            pltpu.VMEM((GROUPS, 1, 128), F32),
            pltpu.VMEM((NY, SLOTS, width), BF16),
            pltpu.VMEM((SLOTS, width), BF16),
            pltpu.VMEM((NY, 1, SLOTS), F32),
            pltpu.VMEM((1, SLOTS), F32),
            pltpu.VMEM((1, SLOTS), F32),
            pltpu.VMEM((1, SLOTS), F32),
            pltpu.VMEM((2, 1, 128), F32),
            pltpu.VMEM((GROUPS, 1, 128), F32),
            pltpu.SemaphoreType.REGULAR,
            sem((3,)),
            sem, sem((CHUNKS,)), sem, sem,
            sem((CHUNKS, 5)), sem((CHUNKS, 5)), sem((NY,)), sem((NY,)),
            sem, sem, sem, sem,
        ],
        compiler_params=pltpu.CompilerParams(
            collective_id=0, has_side_effects=True, vmem_limit_bytes=40 * 1024 * 1024
        ),
    )(embeddings, cluster.reshape(1, rows), rank.reshape(1, rows))
    return out.reshape(rows)


def solution(mesh):
    in_specs = (P(("dp", "grp"), None), P(("dp", "grp"), None), P(("dp", "grp")))
    out_specs = P(("dp", "grp"))
    return jax.shard_map(body, mesh=mesh, in_specs=in_specs, out_specs=out_specs, check_vma=False)
```

```python
import jax
import jax.numpy as jnp
from jax import lax
from jax.experimental import pallas as pl
from jax.experimental.pallas import tpu as pltpu
from jax.sharding import PartitionSpec as P

NX, NY, NZ = 4, 4, 16
GROUPS = NX * NZ
MOST = 4
SLOTS = GROUPS * MOST
EMPTY = 65536.0

REACH = 4
NEAR = [(dx, dz) for dx in (2, 1, 3, 0) for d in range(REACH, 0, -1) for dz in (d, -d)]
NEAR = [place for dx in (2, 1, 3, 0) for place in [n for n in NEAR if n[0] == dx] + [(dx, 0)]]
FAR = [(dx, dz) for dx in (2, 1, 3, 0) for dz in (8, -7, 7, -6, 6, -5, 5)]
FIRST = 28
PLACES = NEAR[:FIRST] + FAR + NEAR[FIRST:]
SPANS = [(0, 16), (16, 28), (28, 44), (44, 56), (56, 64)]
CHUNKS = len(SPANS)
SOON = 3
EARLY = SPANS[SOON][0] * MOST
Z_ORDER = [8, -7, 7, -6, 6, -5, 5, -4, 4, -3, 3, -2, 2, -1, 1, 0]
LAST = GROUPS - 1

F32, BF16 = jnp.float32, jnp.bfloat16


def iota(shape, dim):
    return lax.broadcasted_iota(jnp.int32, shape, dim)


def onehot(cond):
    return jnp.where(cond, 1.0, 0.0)


def dot(a, b):
    return lax.dot_general(a, b, (((1,), (0,)), ((), ())), preferred_element_type=F32)


def kernel(emb_in, lab_in, rank_in, out, emb, lab, rank, S, Sr, R, Rr1, Rr2, K, Q2, D2, KR, QR2, DR2, PM, PMs, BS, V,
           gate, in_s, row_s, row_r, rz_s, rz_r, rx_s, rx_r, y_s, y_r, yr_s, yr_r, pm_s, pm_r, b_s, b_r):
    dp, grp = lax.axis_index("dp"), lax.axis_index("grp")
    x, z = lax.div(dp, NZ), lax.rem(dp, NZ)
    y, core = lax.div(grp, 2), lax.rem(grp, 2)
    z_at = {dz: lax.rem(z + (dz + NZ), NZ) for dz in range(1 - NZ // 2, NZ // 2 + 1)}
    z_from = {dz: lax.rem(z + (NZ - dz), NZ) for dz in z_at}
    x_at = [lax.rem(x + dx, NX) * NZ for dx in range(NX)]
    x_from = [lax.rem(x + (NX - dx), NX) * NZ for dx in range(NX)]
    target = [x_at[dx] + z_at[dz] for dx, dz in PLACES]
    source = [x_from[dx] + z_from[dz] for dx, dz in PLACES]

    up = (dp, lax.rem(y + 1, NY) * 2 + core)
    below = lax.rem(y + (NY - 1), NY) * 2 + core
    down = (dp, below)
    sibling = (dp, y * 2 + 1 - core)
    mesh_id = pl.DeviceIdType.MESH
    started = []

    def send(src, dst, send_sem, recv_sem, to, keep=True):
        copy = pltpu.make_async_remote_copy(
            src_ref=src, dst_ref=dst, send_sem=send_sem, recv_sem=recv_sem, device_id=to, device_id_type=mesh_id
        )
        copy.start()
        if keep:
            started.append(copy)
        return copy

    def wait_all(ref, sem):
        pltpu.make_async_copy(ref, ref, sem).wait()

    barrier = pltpu.get_barrier_semaphore()
    far = [abs(dz) > REACH for _, dz in PLACES]
    peers = [(target[p], y * 2 + int(far[p])) for p in range(LAST)] + [up, down, sibling]
    for peer in peers:
        pl.semaphore_signal(barrier, inc=1, device_id=peer, device_id_type=mesh_id)

    def listen(reach, count):
        @pl.when(core == reach)
        def _():
            pl.semaphore_wait(barrier, 2 * count + 3)
            pl.semaphore_signal(gate, inc=1, device_id=sibling, device_id_type=mesh_id)

        @pl.when(core != reach)
        def _():
            pl.semaphore_wait(gate, 1)

    loads = [pltpu.make_async_copy(a, b, in_s.at[i]) for i, (a, b) in enumerate(
        ((lab_in, lab), (rank_in, rank), (emb_in, emb)))]
    for load in loads:
        load.start()
    loads[0].wait()
    loads[1].wait()

    lab_row = lab[...].astype(F32)
    i0, i1 = iota((128, 128), 0), iota((128, 128), 1)
    lab_all = jnp.broadcast_to(lab_row, (128, 128))
    lab_col = jnp.sum(jnp.where(i0 == i1, lab_all, 0.0), axis=1, keepdims=True)
    same = onehot(lab_col == lab_all)
    slot_row = jnp.sum(jnp.where(i0 < i1, same, 0.0), axis=0, keepdims=True)
    slot_col = jnp.sum(jnp.where(i1 < i0, same, 0.0), axis=1, keepdims=True)
    pos_row = lab_row * MOST + slot_row

    rank_row = rank[...].astype(F32)
    high = jnp.floor(rank_row * (1.0 / 256))
    low = rank_row - 256.0 * high
    xg_row = jnp.floor(lab_row * (1.0 / NZ))
    xg_col = jnp.floor(lab_col * (1.0 / NZ))
    mine = lab_row - NZ * xg_row == iota((NZ, 128), 0).astype(F32)
    parts = jnp.concatenate(
        [jnp.where(mine, high, 0.0), jnp.where(mine, low, 0.0), onehot(mine)], axis=0
    ).astype(BF16)
    place = onehot(xg_col * MOST + slot_col == i1.astype(F32)).astype(BF16)
    found = dot(parts, place)
    ranks = found[:NZ] * 256.0 + found[NZ:2 * NZ] + (1.0 - found[2 * NZ:]) * EMPTY
    for i in range(NZ):
        Sr[i] = ranks[i:i + 1]

    width = emb.shape[1]
    half = width // 2
    s0, s1 = iota((2 * SLOTS, 256), 0), iota((2 * SLOTS, 256), 1)
    slot_of = (s0 // 8) * MOST + s0 % MOST
    pos_two = jnp.concatenate([pos_row, pos_row], axis=1)
    spread = onehot((pos_two == slot_of.astype(F32)) & ((s0 // MOST) % 2 == s1 // 128)).astype(BF16)
    loads[2].wait()
    values = emb[...].astype(F32)
    scale = lax.rsqrt(jnp.mean(values * values, axis=1, keepdims=True) + 1e-06) / jnp.sqrt(F32(width))
    unit = (values * scale).astype(BF16)
    S[...] = dot(spread, jnp.concatenate([unit[:, :half], unit[:, half:]], axis=0)).astype(BF16).reshape(S.shape)

    chunk_of = [t for t, (lo, hi) in enumerate(SPANS) for _ in range(lo, hi)]

    def send_rows(places):
        for p in places:
            send(S.at[target[p]], R.at[p], row_s, row_r.at[chunk_of[p]], (target[p], grp), False)

    def send_ranks(distant):
        for i, dz in enumerate(Z_ORDER[:NZ - 1]):
            if (abs(dz) > REACH) == distant:
                send(Sr.at[z_at[dz]], Rr1.at[i], rz_s, rz_r, (x * NZ + z_at[dz], grp), False)

    listen(0, LAST - sum(far))
    send_rows(range(FIRST))
    send_ranks(False)
    listen(1, sum(far))
    send_ranks(True)
    send_rows(range(FIRST, LAST))
    R[LAST] = S[dp]
    Rr1[NZ - 1] = Sr[z]

    from_down, from_up, to_q2, to_d2 = {}, {}, {}, {}

    def span(t):
        lo, hi = SPANS[t]
        return lo, hi - lo, pl.ds(lo * MOST, (hi - lo) * MOST)

    def arrive(t):
        lo, places, at = span(t)
        wait_all(R.at[pl.ds(lo, places - (t == CHUNKS - 1))], row_r.at[t])
        count = places * MOST
        o0, o1 = iota((2 * count, 2 * count), 0), iota((2 * count, 2 * count), 1)
        whole = onehot(o1 == ((o0 % count) // MOST) * 8 + (o0 // count) * MOST + o0 % MOST).astype(BF16)
        rows = dot(whole, R[lo:lo + places].reshape(2 * count, half)).astype(BF16)
        K[0, lo * MOST:lo * MOST + count, :half] = rows[:count]
        K[0, lo * MOST:lo * MOST + count, half:] = rows[count:]
        from_down[t] = send(K.at[0, at], K.at[2, at], y_s.at[t, 0], y_r.at[t, 0], up)
        from_up[t] = send(K.at[0, at], K.at[1, at], y_s.at[t, 1], y_r.at[t, 1], down)
        to_q2[t] = send(K.at[0, at], Q2.at[at], y_s.at[t, 2], y_r.at[t, 2], sibling)

    def share(t):
        _, _, at = span(t)
        from_down[t].wait_recv()
        to_d2[t] = send(K.at[2, at], D2.at[at], y_s.at[t, 3], y_r.at[t, 3], sibling)

    arrive(0)
    arrive(1)
    share(0)
    share(1)

    wait_all(Rr1.at[pl.ds(0, NZ - 1)], rz_r)
    rx_copy = []
    for dx in range(1, NX):
        rx_copy.append(send(Rr1, Rr2.at[dx], rx_s.at[dx], rx_r.at[dx], (x_at[dx] + z, grp)))
    Rr2[0] = Rr1[...]
    for copy in rx_copy:
        copy.wait_recv()
    lanes = Rr2[...].reshape(GROUPS, 128)
    lane_high = jnp.floor(lanes * (1.0 / 256))
    lane_low = lanes - 256.0 * lane_high
    column = [dx * NZ + Z_ORDER.index(dz) for dx, dz in PLACES]
    r8, g1 = iota((8, GROUPS), 0), iota((8, GROUPS), 1)
    pick = jnp.concatenate(
        [onehot(g1 == jnp.where(r8 < MOST, column[p], column[p + 1])) for p in range(0, GROUPS, 2)], axis=0
    ).astype(BF16)
    both = dot(pick, jnp.concatenate([lane_high, lane_low], axis=1).astype(BF16))
    wide = both[:, :128] * 256.0 + both[:, 128:]
    w0, w1 = iota((SLOTS, 128), 0), iota((SLOTS, 128), 1)
    own_col = jnp.sum(jnp.where(w1 == x * MOST + w0 % MOST, wide, 0.0), axis=1, keepdims=True)
    d0, d1 = iota((SLOTS, SLOTS), 0), iota((SLOTS, SLOTS), 1)
    KR[0] = jnp.sum(jnp.where(d0 == d1, own_col, 0.0), axis=0, keepdims=True)
    yr_copy = [
        send(KR.at[0], KR.at[2], yr_s.at[0], yr_r.at[0], up),
        send(KR.at[0], KR.at[1], yr_s.at[1], yr_r.at[1], down),
        send(KR.at[0], QR2, yr_s.at[2], yr_r.at[2], sibling),
    ]
    for copy in yr_copy:
        copy.wait_recv()
    dr_copy = send(KR.at[2], DR2, yr_s.at[3], yr_r.at[3], sibling)

    arrive(2)
    arrive(3)
    arrive(4)

    rows8 = iota((8, 128), 0)
    cluster_of = []
    for p in range(0, GROUPS, 8):
        block = jnp.zeros((8, 128), jnp.int32)
        for i in range(8):
            block = jnp.where(rows8 == i, target[p + i], block)
        cluster_of.append(block)
    cluster_of = jnp.concatenate(cluster_of, axis=0).astype(F32)

    def cosines(best, keys, key_rank, queries, ranks_q):
        cosine = lax.dot_general(keys, queries, (((1,), (1,)), ((), ())), preferred_element_type=F32)
        masked = jnp.where(key_rank < ranks_q, cosine, -jnp.inf)
        return jnp.maximum(best, jnp.max(masked, axis=0, keepdims=True))

    dr_copy.wait_recv()
    query_rank = [KR[0], QR2[...], KR[2], DR2[...]]
    query = [K.at[0], Q2, K.at[2], D2]
    key_rank = [jnp.sum(jnp.where(d0 == d1, KR[b], 0.0), axis=1, keepdims=True) for b in range(3)]
    pairs = [(0, 0), (0, 1), (1, 0), (1, 1), (2, 0), (2, 1), (1, 2), (1, 3)]
    early = [jnp.full((1, EARLY), -1.0, F32)] * 4
    late = [jnp.full((1, SLOTS - EARLY), -1.0, F32)] * 4
    best = [jnp.full((1, SLOTS), -1.0, F32)] * 4

    for t in range(SOON):
        if t == SOON - 1:
            share(t)
        from_up[t].wait_recv()
        to_q2[t].wait_recv()
        to_d2[t].wait_recv()
    for b, c in pairs:
        early[c] = cosines(early[c], K[b, :EARLY], key_rank[b][:EARLY], query[c][:EARLY], query_rank[c][:, :EARLY])
    for t in range(SOON, CHUNKS):
        share(t)
        from_up[t].wait_recv()
        to_q2[t].wait_recv()
    for b, c in pairs:
        if c == 3:
            for t in range(SOON, CHUNKS):
                to_d2[t].wait_recv()
        late[c] = cosines(late[c], K[b, :EARLY], key_rank[b][:EARLY], query[c][EARLY:], query_rank[c][:, EARLY:])
        best[c] = cosines(best[c], K[b, EARLY:], key_rank[b][EARLY:], query[c][...], query_rank[c])
    best = [jnp.maximum(best[c], jnp.concatenate([early[c], late[c]], axis=1)) for c in range(4)]

    PMs[:, :SLOTS] = best[1]
    PMs[:, SLOTS:] = best[3]
    send(PMs, PM, pm_s, pm_r, sibling).wait_recv()
    own = jnp.maximum(best[0], PM[:, :SLOTS])
    lower = jnp.maximum(best[2], PM[:, SLOTS:])
    for i in range(2):
        BS[i] = own[:, i * 128:(i + 1) * 128]
        BS[2 + i] = lower[:, i * 128:(i + 1) * 128]

    hops = [min(dx, NX - dx) + abs(dz) for dx, dz in PLACES]
    for p in sorted(range(GROUPS), key=lambda p: -hops[p]):
        send(BS.at[2 + p // 32], V.at[GROUPS + p], b_s.at[1], b_r.at[1], (source[p], below), False)
        if p < LAST:
            send(BS.at[p // 32], V.at[p], b_s.at[0], b_r.at[0], (source[p], grp), False)
    V[LAST] = BS[1]
    a0, a1 = iota((GROUPS, 128), 0), iota((GROUPS, 128), 1)
    first = (a0 % 32) * MOST
    wait_all(V.at[pl.ds(0, LAST)], b_r.at[0])
    wait_all(V.at[pl.ds(GROUPS, GROUPS)], b_r.at[1])
    back = jnp.maximum(V[:GROUPS], V[GROUPS:]).reshape(GROUPS, 128)
    held = jnp.where((a1 >= first) & (a1 < first + MOST), back, 0.0)
    shift = 64
    while shift >= MOST:
        held = held + pltpu.roll(held, shift, 1)
        shift //= 2
    chosen = jnp.zeros((GROUPS, 128), F32)
    for s in range(MOST):
        hit = (cluster_of == lab_row) & (slot_row == float(s))
        chosen = chosen + jnp.where(hit, held[:, s:s + 1], 0.0)
    out[...] = jnp.sum(chosen, axis=0, keepdims=True)

    wait_all(R.at[pl.ds(0, LAST)], row_s)
    wait_all(Rr1.at[pl.ds(0, NZ - 1)], rz_s)
    wait_all(V.at[pl.ds(0, LAST)], b_s.at[0])
    wait_all(V.at[pl.ds(GROUPS, GROUPS)], b_s.at[1])
    for copy in started:
        copy.wait_send()


def body(embeddings, cluster, rank):
    rows, width = embeddings.shape
    sem = pltpu.SemaphoreType.DMA
    out = pl.pallas_call(
        kernel,
        out_shape=jax.ShapeDtypeStruct((1, rows), F32),
        in_specs=[pl.BlockSpec(memory_space=pl.ANY)] * 3,
        out_specs=pl.BlockSpec(memory_space=pltpu.VMEM),
        scratch_shapes=[
            pltpu.VMEM((rows, width), BF16),
            pltpu.VMEM((1, rows), jnp.int32),
            pltpu.VMEM((1, rows), jnp.int32),
            pltpu.VMEM((GROUPS, 8, width // 2), BF16),
            pltpu.VMEM((NZ, 1, 128), F32),
            pltpu.VMEM((GROUPS, 8, width // 2), BF16),
            pltpu.VMEM((NZ, 1, 128), F32),
            pltpu.VMEM((NX, NZ, 1, 128), F32),
            pltpu.VMEM((3, SLOTS, width), BF16),
            pltpu.VMEM((SLOTS, width), BF16),
            pltpu.VMEM((SLOTS, width), BF16),
            pltpu.VMEM((3, 1, SLOTS), F32),
            pltpu.VMEM((1, SLOTS), F32),
            pltpu.VMEM((1, SLOTS), F32),
            pltpu.VMEM((1, 2 * SLOTS), F32),
            pltpu.VMEM((1, 2 * SLOTS), F32),
            pltpu.VMEM((4, 1, 128), F32),
            pltpu.VMEM((2 * GROUPS, 1, 128), F32),
            pltpu.SemaphoreType.REGULAR,
            sem((3,)),
            sem, sem((CHUNKS,)), sem, sem, sem((NX,)), sem((NX,)),
            sem((CHUNKS, 4)), sem((CHUNKS, 4)), sem((4,)), sem((4,)),
            sem, sem, sem((2,)), sem((2,)),
        ],
        compiler_params=pltpu.CompilerParams(
            collective_id=0, has_side_effects=True, vmem_limit_bytes=40 * 1024 * 1024
        ),
    )(embeddings, cluster.reshape(1, rows), rank.reshape(1, rows))
    return out.reshape(rows)


def solution(mesh):
    in_specs = (P(("dp", "grp"), None), P(("dp", "grp"), None), P(("dp", "grp")))
    out_specs = P(("dp", "grp"))
    return jax.shard_map(body, mesh=mesh, in_specs=in_specs, out_specs=out_specs, check_vma=False)
```

```python
import jax
import jax.numpy as jnp
from jax import lax
from jax.experimental import pallas as pl
from jax.experimental.pallas import tpu as pltpu
from jax.sharding import PartitionSpec as P

NX, NY, NZ = 4, 4, 16
GROUPS = NX * NZ
MOST = 4
SLOTS = GROUPS * MOST
EMPTY = 65536.0

LAST = GROUPS - 1
REACH = 4
DZ_NEAR = [4, -4, 3, -3, 2, -2, 1, -1, 0]
DZ_FAR = [8, -7, 7, -6, 6, -5, 5]
NEAR = [(dx, dz) for dx in (2, 1, 3, 0) for dz in DZ_NEAR][:-1]
PLACES = NEAR + [(dx, dz) for dx in (2, 1, 3, 0) for dz in DZ_FAR] + [(0, 0)]
FIRST = len(NEAR)
SPANS = [(0, 16), (16, 32), (32, 40), (40, 48), (48, 56), (56, 64)]
WINDOWS = [(0, FIRST), (FIRST, 40), (40, 48), (48, 56), (56, LAST)]
CHUNKS = len(SPANS)
Z_ORDER = [8, -7, 7, -6, 6, -5, 5, -4, 4, -3, 3, -2, 2, -1, 1, 0]

F32, BF16 = jnp.float32, jnp.bfloat16


def iota(shape, dim):
    return lax.broadcasted_iota(jnp.int32, shape, dim)


def onehot(cond):
    return jnp.where(cond, 1.0, 0.0)


def dot(a, b):
    return lax.dot_general(a, b, (((1,), (0,)), ((), ())), preferred_element_type=F32)


def kernel(emb_in, lab_in, rank_in, out, emb, lab, rank, S, Sr, R, Rr1, Rr2, K, Q2, D2, KR, QR2, DR2, PM, PMs, BS, V,
           gate, in_s, row_s, row_r, rz_s, rz_r, rx_s, rx_r, y_s, y_r, yr_s, yr_r, pm_s, pm_r, b_s, b_r):
    dp, grp = lax.axis_index("dp"), lax.axis_index("grp")
    x, z = lax.div(dp, NZ), lax.rem(dp, NZ)
    y, core = lax.div(grp, 2), lax.rem(grp, 2)
    z_at = {dz: lax.rem(z + (dz + NZ), NZ) for dz in range(1 - NZ // 2, NZ // 2 + 1)}
    z_from = {dz: lax.rem(z + (NZ - dz), NZ) for dz in z_at}
    x_at = [lax.rem(x + dx, NX) * NZ for dx in range(NX)]
    x_from = [lax.rem(x + (NX - dx), NX) * NZ for dx in range(NX)]
    target = [x_at[dx] + z_at[dz] for dx, dz in PLACES]
    source = [x_from[dx] + z_from[dz] for dx, dz in PLACES]

    up = (dp, lax.rem(y + 1, NY) * 2 + core)
    below = lax.rem(y + (NY - 1), NY) * 2 + core
    down = (dp, below)
    sibling = (dp, y * 2 + 1 - core)
    mesh_id = pl.DeviceIdType.MESH
    started = []

    def send(src, dst, send_sem, recv_sem, to, keep=True):
        copy = pltpu.make_async_remote_copy(
            src_ref=src, dst_ref=dst, send_sem=send_sem, recv_sem=recv_sem, device_id=to, device_id_type=mesh_id
        )
        copy.start()
        if keep:
            started.append(copy)
        return copy

    def wait_all(ref, sem):
        pltpu.make_async_copy(ref, ref, sem).wait()

    barrier = pltpu.get_barrier_semaphore()
    far = [abs(dz) > REACH for _, dz in PLACES]
    peers = [(target[p], y * 2 + int(far[p])) for p in range(LAST)] + [up, down, sibling]
    for peer in peers:
        pl.semaphore_signal(barrier, inc=1, device_id=peer, device_id_type=mesh_id)

    def listen(reach, count):
        @pl.when(core == reach)
        def _():
            pl.semaphore_wait(barrier, 2 * count + 3)
            pl.semaphore_signal(gate, inc=1, device_id=sibling, device_id_type=mesh_id)

        @pl.when(core != reach)
        def _():
            pl.semaphore_wait(gate, 1)

    loads = [pltpu.make_async_copy(a, b, in_s.at[i]) for i, (a, b) in enumerate(
        ((lab_in, lab), (rank_in, rank), (emb_in, emb)))]
    for load in loads:
        load.start()
    loads[0].wait()
    loads[1].wait()

    lab_row = lab[...].astype(F32)
    i0, i1 = iota((128, 128), 0), iota((128, 128), 1)
    lab_all = jnp.broadcast_to(lab_row, (128, 128))
    lab_col = jnp.sum(jnp.where(i0 == i1, lab_all, 0.0), axis=1, keepdims=True)
    same = onehot(lab_col == lab_all)
    slot_row = jnp.sum(jnp.where(i0 < i1, same, 0.0), axis=0, keepdims=True)
    slot_col = jnp.sum(jnp.where(i1 < i0, same, 0.0), axis=1, keepdims=True)
    pos_row = lab_row * MOST + slot_row

    rank_row = rank[...].astype(F32)
    high = jnp.floor(rank_row * (1.0 / 256))
    low = rank_row - 256.0 * high
    xg_row = jnp.floor(lab_row * (1.0 / NZ))
    xg_col = jnp.floor(lab_col * (1.0 / NZ))
    mine = lab_row - NZ * xg_row == iota((NZ, 128), 0).astype(F32)
    parts = jnp.concatenate(
        [jnp.where(mine, high, 0.0), jnp.where(mine, low, 0.0), onehot(mine)], axis=0
    ).astype(BF16)
    place = onehot(xg_col * MOST + slot_col == i1.astype(F32)).astype(BF16)
    found = dot(parts, place)
    ranks = found[:NZ] * 256.0 + found[NZ:2 * NZ] + (1.0 - found[2 * NZ:]) * EMPTY
    for i in range(NZ):
        Sr[i] = ranks[i:i + 1]

    width = emb.shape[1]
    half = width // 2
    s0, s1 = iota((2 * SLOTS, 256), 0), iota((2 * SLOTS, 256), 1)
    slot_of = (s0 // 8) * MOST + s0 % MOST
    pos_two = jnp.concatenate([pos_row, pos_row], axis=1)
    spread = onehot((pos_two == slot_of.astype(F32)) & ((s0 // MOST) % 2 == s1 // 128)).astype(BF16)
    loads[2].wait()
    values = emb[...].astype(F32)
    scale = lax.rsqrt(jnp.mean(values * values, axis=1, keepdims=True) + 1e-06) / jnp.sqrt(F32(width))
    unit = (values * scale).astype(BF16)
    S[...] = dot(spread, jnp.concatenate([unit[:, :half], unit[:, half:]], axis=0)).astype(BF16).reshape(S.shape)

    chunk_of = [t for t, (lo, hi) in enumerate(SPANS) for _ in range(lo, hi)]

    window_of = [w for w, (lo, hi) in enumerate(WINDOWS) for _ in range(lo, hi)]

    def sent(w):
        lo, hi = WINDOWS[w]
        wait_all(R.at[pl.ds(lo, hi - lo)], row_s.at[w])

    def send_rows(places):
        for p in places:
            send(S.at[target[p]], R.at[p], row_s.at[window_of[p]], row_r.at[chunk_of[p]], (target[p], grp), False)

    def send_ranks(distant):
        for i, dz in enumerate(Z_ORDER[:NZ - 1]):
            if (abs(dz) > REACH) == distant:
                send(Sr.at[z_at[dz]], Rr1.at[i], rz_s, rz_r, (x * NZ + z_at[dz], grp), False)

    listen(0, LAST - sum(far))
    send_rows(range(FIRST))
    send_ranks(False)
    listen(1, sum(far))
    send_ranks(True)
    send_rows(range(FIRST, 48))
    R[LAST] = S[dp]
    Rr1[NZ - 1] = Sr[z]

    from_down, from_up, to_q2, to_d2 = {}, {}, {}, {}

    def span(t):
        lo, hi = SPANS[t]
        return lo, hi - lo, pl.ds(lo * MOST, (hi - lo) * MOST)

    def arrive(t):
        lo, places, at = span(t)
        wait_all(R.at[pl.ds(lo, places - (t == CHUNKS - 1))], row_r.at[t])
        count = places * MOST
        o0, o1 = iota((2 * count, 2 * count), 0), iota((2 * count, 2 * count), 1)
        whole = onehot(o1 == ((o0 % count) // MOST) * 8 + (o0 // count) * MOST + o0 % MOST).astype(BF16)
        rows = dot(whole, R[lo:lo + places].reshape(2 * count, half)).astype(BF16)
        K[0, lo * MOST:lo * MOST + count, :half] = rows[:count]
        K[0, lo * MOST:lo * MOST + count, half:] = rows[count:]
        from_down[t] = send(K.at[0, at], K.at[2, at], y_s.at[t, 0], y_r.at[t, 0], up)
        from_up[t] = send(K.at[0, at], K.at[1, at], y_s.at[t, 1], y_r.at[t, 1], down)
        to_q2[t] = send(K.at[0, at], Q2.at[at], y_s.at[t, 2], y_r.at[t, 2], sibling)

    def share(t):
        _, _, at = span(t)
        from_down[t].wait_recv()
        to_d2[t] = send(K.at[2, at], D2.at[at], y_s.at[t, 3], y_r.at[t, 3], sibling)

    arrive(0)
    sent(1)
    send_rows(range(48, 56))
    arrive(1)
    sent(2)
    send_rows(range(56, LAST))

    wait_all(Rr1.at[pl.ds(0, NZ - 1)], rz_r)
    rx_copy = []
    for dx in range(1, NX):
        rx_copy.append(send(Rr1, Rr2.at[dx], rx_s.at[dx], rx_r.at[dx], (x_at[dx] + z, grp)))
    Rr2[0] = Rr1[...]
    share(0)
    share(1)
    arrive(2)
    for copy in rx_copy:
        copy.wait_recv()
    lanes = Rr2[...].reshape(GROUPS, 128)
    lane_high = jnp.floor(lanes * (1.0 / 256))
    lane_low = lanes - 256.0 * lane_high
    column = [dx * NZ + Z_ORDER.index(dz) for dx, dz in PLACES]
    r8, g1 = iota((8, GROUPS), 0), iota((8, GROUPS), 1)
    pick = jnp.concatenate(
        [onehot(g1 == jnp.where(r8 < MOST, column[p], column[p + 1])) for p in range(0, GROUPS, 2)], axis=0
    ).astype(BF16)
    both = dot(pick, jnp.concatenate([lane_high, lane_low], axis=1).astype(BF16))
    wide = both[:, :128] * 256.0 + both[:, 128:]
    w0, w1 = iota((SLOTS, 128), 0), iota((SLOTS, 128), 1)
    own_col = jnp.sum(jnp.where(w1 == x * MOST + w0 % MOST, wide, 0.0), axis=1, keepdims=True)
    d0, d1 = iota((SLOTS, SLOTS), 0), iota((SLOTS, SLOTS), 1)
    KR[0] = jnp.sum(jnp.where(d0 == d1, own_col, 0.0), axis=0, keepdims=True)
    yr_copy = [
        send(KR.at[0], KR.at[2], yr_s.at[0], yr_r.at[0], up),
        send(KR.at[0], KR.at[1], yr_s.at[1], yr_r.at[1], down),
        send(KR.at[0], QR2, yr_s.at[2], yr_r.at[2], sibling),
    ]

    arrive(3)
    rows8 = iota((8, 128), 0)
    cluster_of = []
    for p in range(0, GROUPS, 8):
        block = jnp.zeros((8, 128), jnp.int32)
        for i in range(8):
            block = jnp.where(rows8 == i, target[p + i], block)
        cluster_of.append(block)
    cluster_of = jnp.concatenate(cluster_of, axis=0).astype(F32)

    arrive(4)
    for copy in yr_copy:
        copy.wait_recv()
    dr_copy = send(KR.at[2], DR2, yr_s.at[3], yr_r.at[3], sibling)
    key_rank = [jnp.sum(jnp.where(d0 == d1, KR[b], 0.0), axis=1, keepdims=True) for b in range(3)]
    arrive(5)
    for t in range(2, CHUNKS):
        share(t)
    dr_copy.wait_recv()
    query_rank = [KR[0], QR2[...], KR[2], DR2[...]]
    query = [K.at[0], Q2, K.at[2], D2]

    def largest(c, chips):
        best = jnp.full((1, SLOTS), -1.0, F32)
        for b in chips:
            cosine = lax.dot_general(K[b], query[c][...], (((1,), (1,)), ((), ())), preferred_element_type=F32)
            masked = jnp.where(key_rank[b] < query_rank[c], cosine, -jnp.inf)
            best = jnp.maximum(best, jnp.max(masked, axis=0, keepdims=True))
        return best

    for t in range(CHUNKS):
        from_up[t].wait_recv()
    lower = largest(2, (1,))
    for t in range(CHUNKS):
        to_d2[t].wait_recv()
    PMs[1] = largest(3, (1,))
    pm_lower = send(PMs.at[1], PM.at[1], pm_s.at[1], pm_r.at[1], sibling)
    for t in range(CHUNKS):
        to_q2[t].wait_recv()
    PMs[0] = largest(1, range(3))
    pm_own = send(PMs.at[0], PM.at[0], pm_s.at[0], pm_r.at[0], sibling)
    own = largest(0, range(3))

    hops = [min(dx, NX - dx) + abs(dz) for dx, dz in PLACES]
    far_first = sorted(range(GROUPS), key=lambda p: -hops[p])
    pm_lower.wait_recv()
    lower = jnp.maximum(lower, PM[1])
    for i in range(2):
        BS[2 + i] = lower[:, i * 128:(i + 1) * 128]
    for p in far_first:
        send(BS.at[2 + p // 32], V.at[GROUPS + p], b_s.at[1], b_r.at[1], (source[p], below), False)
    pm_own.wait_recv()
    own = jnp.maximum(own, PM[0])
    for i in range(2):
        BS[i] = own[:, i * 128:(i + 1) * 128]
    for p in far_first:
        if p < LAST:
            send(BS.at[p // 32], V.at[p], b_s.at[0], b_r.at[0], (source[p], grp), False)
    V[LAST] = BS[1]
    a0, a1 = iota((GROUPS, 128), 0), iota((GROUPS, 128), 1)
    first = (a0 % 32) * MOST
    wait_all(V.at[pl.ds(0, LAST)], b_r.at[0])
    wait_all(V.at[pl.ds(GROUPS, GROUPS)], b_r.at[1])
    back = jnp.maximum(V[:GROUPS], V[GROUPS:]).reshape(GROUPS, 128)
    held = jnp.where((a1 >= first) & (a1 < first + MOST), back, 0.0)
    shift = 64
    while shift >= MOST:
        held = held + pltpu.roll(held, shift, 1)
        shift //= 2
    chosen = jnp.zeros((GROUPS, 128), F32)
    for s in range(MOST):
        hit = (cluster_of == lab_row) & (slot_row == float(s))
        chosen = chosen + jnp.where(hit, held[:, s:s + 1], 0.0)
    out[...] = jnp.sum(chosen, axis=0, keepdims=True)

    for w in (0, 3, 4):
        sent(w)
    wait_all(Rr1.at[pl.ds(0, NZ - 1)], rz_s)
    wait_all(V.at[pl.ds(0, LAST)], b_s.at[0])
    wait_all(V.at[pl.ds(GROUPS, GROUPS)], b_s.at[1])
    for copy in started:
        copy.wait_send()


def body(embeddings, cluster, rank):
    rows, width = embeddings.shape
    sem = pltpu.SemaphoreType.DMA
    out = pl.pallas_call(
        kernel,
        out_shape=jax.ShapeDtypeStruct((1, rows), F32),
        in_specs=[pl.BlockSpec(memory_space=pltpu.HBM)] * 3,
        out_specs=pl.BlockSpec(memory_space=pltpu.VMEM),
        scratch_shapes=[
            pltpu.VMEM((rows, width), BF16),
            pltpu.VMEM((1, rows), jnp.int32),
            pltpu.VMEM((1, rows), jnp.int32),
            pltpu.VMEM((GROUPS, 8, width // 2), BF16),
            pltpu.VMEM((NZ, 1, 128), F32),
            pltpu.VMEM((GROUPS, 8, width // 2), BF16),
            pltpu.VMEM((NZ, 1, 128), F32),
            pltpu.VMEM((NX, NZ, 1, 128), F32),
            pltpu.VMEM((3, SLOTS, width), BF16),
            pltpu.VMEM((SLOTS, width), BF16),
            pltpu.VMEM((SLOTS, width), BF16),
            pltpu.VMEM((3, 1, SLOTS), F32),
            pltpu.VMEM((1, SLOTS), F32),
            pltpu.VMEM((1, SLOTS), F32),
            pltpu.VMEM((2, 1, SLOTS), F32),
            pltpu.VMEM((2, 1, SLOTS), F32),
            pltpu.VMEM((4, 1, 128), F32),
            pltpu.VMEM((2 * GROUPS, 1, 128), F32),
            pltpu.SemaphoreType.REGULAR,
            sem((3,)),
            sem((len(WINDOWS),)), sem((CHUNKS,)), sem, sem, sem((NX,)), sem((NX,)),
            sem((CHUNKS, 4)), sem((CHUNKS, 4)), sem((4,)), sem((4,)),
            sem((2,)), sem((2,)), sem((2,)), sem((2,)),
        ],
        compiler_params=pltpu.CompilerParams(
            collective_id=0, has_side_effects=True, vmem_limit_bytes=40 * 1024 * 1024
        ),
    )(*(pltpu.with_memory_space_constraint(a, pltpu.HBM) for a in (embeddings, cluster.reshape(1, rows), rank.reshape(1, rows))))
    return out.reshape(rows)


def solution(mesh):
    in_specs = (P(("dp", "grp"), None), P(("dp", "grp"), None), P(("dp", "grp")))
    out_specs = P(("dp", "grp"))
    return jax.shard_map(body, mesh=mesh, in_specs=in_specs, out_specs=out_specs, check_vma=False)
```

```python
import jax
import jax.numpy as jnp
from jax import lax
from jax.experimental import pallas as pl
from jax.experimental.pallas import tpu as pltpu
from jax.sharding import PartitionSpec as P

NX, NY, NZ = 4, 4, 16
GROUPS = NX * NZ
MOST = 4
SLOTS = GROUPS * MOST
EMPTY = 65536.0

REACH = 4
DZ_NEAR = [4, -4, 3, -3, 2, -2, 1, -1, 0]
DZ_FAR = [8, -7, 7, -6, 6, -5, 5]
NEAR = [(dx, dz) for dx in (2, 1, 3, 0) for dz in DZ_NEAR][:-1]
PLACES = NEAR + [(dx, dz) for dx in (2, 1, 3, 0) for dz in DZ_FAR] + [(0, 0)]
FIRST = len(NEAR)
SPANS = [(0, 16), (16, 32), (32, 40), (40, 48), (48, 56), (56, 64)]
CHUNKS = len(SPANS)
Z_ORDER = [8, -7, 7, -6, 6, -5, 5, -4, 4, -3, 3, -2, 2, -1, 1, 0]
LAST = GROUPS - 1

F32, BF16 = jnp.float32, jnp.bfloat16


def iota(shape, dim):
    return lax.broadcasted_iota(jnp.int32, shape, dim)


def onehot(cond):
    return jnp.where(cond, 1.0, 0.0)


def dot(a, b):
    return lax.dot_general(a, b, (((1,), (0,)), ((), ())), preferred_element_type=F32)


def kernel(emb_in, lab_in, rank_in, out, emb, lab, rank, S, Sr, R, Rr1, Rr2, K, Q2, D2, KR, QR2, DR2, PM, PMs, BS, V,
           gate, in_s, row_s, row_r, rz_s, rz_r, rx_s, rx_r, y_s, y_r, yr_s, yr_r, pm_s, pm_r, b_s, b_r):
    dp, grp = lax.axis_index("dp"), lax.axis_index("grp")
    x, z = lax.div(dp, NZ), lax.rem(dp, NZ)
    y, core = lax.div(grp, 2), lax.rem(grp, 2)
    z_at = {dz: lax.rem(z + (dz + NZ), NZ) for dz in range(1 - NZ // 2, NZ // 2 + 1)}
    z_from = {dz: lax.rem(z + (NZ - dz), NZ) for dz in z_at}
    x_at = [lax.rem(x + dx, NX) * NZ for dx in range(NX)]
    x_from = [lax.rem(x + (NX - dx), NX) * NZ for dx in range(NX)]
    target = [x_at[dx] + z_at[dz] for dx, dz in PLACES]
    source = [x_from[dx] + z_from[dz] for dx, dz in PLACES]

    up = (dp, lax.rem(y + 1, NY) * 2 + core)
    below = lax.rem(y + (NY - 1), NY) * 2 + core
    down = (dp, below)
    sibling = (dp, y * 2 + 1 - core)
    mesh_id = pl.DeviceIdType.MESH
    started = []

    def send(src, dst, send_sem, recv_sem, to, keep=True):
        copy = pltpu.make_async_remote_copy(
            src_ref=src, dst_ref=dst, send_sem=send_sem, recv_sem=recv_sem, device_id=to, device_id_type=mesh_id
        )
        copy.start()
        if keep:
            started.append(copy)
        return copy

    def wait_all(ref, sem):
        pltpu.make_async_copy(ref, ref, sem).wait()

    barrier = pltpu.get_barrier_semaphore()
    far = [abs(dz) > REACH for _, dz in PLACES]
    peers = [(target[p], y * 2 + int(far[p])) for p in range(LAST)] + [up, down, sibling]
    distance = [min(dx, NX - dx) + abs(dz) for dx, dz in PLACES]
    peers[:LAST] = [peers[p] for p in sorted(range(LAST), key=lambda p: -distance[p])]
    for peer in peers:
        pl.semaphore_signal(barrier, inc=1, device_id=peer, device_id_type=mesh_id)

    def listen(reach, count):
        @pl.when(core == reach)
        def _():
            pl.semaphore_wait(barrier, 2 * count + 3)
            pl.semaphore_signal(gate, inc=1, device_id=sibling, device_id_type=mesh_id)

        @pl.when(core != reach)
        def _():
            pl.semaphore_wait(gate, 1)

    loads = [pltpu.make_async_copy(a, b, in_s.at[i]) for i, (a, b) in enumerate(
        ((lab_in, lab), (rank_in, rank), (emb_in, emb)))]
    for load in loads:
        load.start()
    loads[0].wait()
    loads[1].wait()

    lab_row = lab[...].astype(F32)
    i0, i1 = iota((128, 128), 0), iota((128, 128), 1)
    lab_all = jnp.broadcast_to(lab_row, (128, 128))
    lab_col = jnp.sum(jnp.where(i0 == i1, lab_all, 0.0), axis=1, keepdims=True)
    same = onehot(lab_col == lab_all)
    slot_row = jnp.sum(jnp.where(i0 < i1, same, 0.0), axis=0, keepdims=True)
    slot_col = jnp.sum(jnp.where(i1 < i0, same, 0.0), axis=1, keepdims=True)
    pos_row = lab_row * MOST + slot_row

    rank_row = rank[...].astype(F32)
    high = jnp.floor(rank_row * (1.0 / 256))
    low = rank_row - 256.0 * high
    xg_row = jnp.floor(lab_row * (1.0 / NZ))
    xg_col = jnp.floor(lab_col * (1.0 / NZ))
    mine = lab_row - NZ * xg_row == iota((NZ, 128), 0).astype(F32)
    parts = jnp.concatenate(
        [jnp.where(mine, high, 0.0), jnp.where(mine, low, 0.0), onehot(mine)], axis=0
    ).astype(BF16)
    place = onehot(xg_col * MOST + slot_col == i1.astype(F32)).astype(BF16)
    found = dot(parts, place)
    ranks = found[:NZ] * 256.0 + found[NZ:2 * NZ] + (1.0 - found[2 * NZ:]) * EMPTY
    for i in range(NZ):
        Sr[i] = ranks[i:i + 1]

    width = emb.shape[1]
    half = width // 2
    s0, s1 = iota((2 * SLOTS, 256), 0), iota((2 * SLOTS, 256), 1)
    slot_of = (s0 // 8) * MOST + s0 % MOST
    pos_two = jnp.concatenate([pos_row, pos_row], axis=1)
    spread = onehot((pos_two == slot_of.astype(F32)) & ((s0 // MOST) % 2 == s1 // 128)).astype(BF16)
    loads[2].wait()
    values = emb[...].astype(F32)
    scale = lax.rsqrt(jnp.mean(values * values, axis=1, keepdims=True) + 1e-06) / jnp.sqrt(F32(width))
    unit = (values * scale).astype(BF16)
    S[...] = dot(spread, jnp.concatenate([unit[:, :half], unit[:, half:]], axis=0)).astype(BF16).reshape(S.shape)

    chunk_of = [t for t, (lo, hi) in enumerate(SPANS) for _ in range(lo, hi)]

    def send_rows(places):
        for p in places:
            send(S.at[target[p]], R.at[p], row_s, row_r.at[chunk_of[p]], (target[p], grp), False)

    def send_ranks(distant):
        for i, dz in enumerate(Z_ORDER[:NZ - 1]):
            if (abs(dz) > REACH) == distant:
                send(Sr.at[z_at[dz]], Rr1.at[i], rz_s, rz_r, (x * NZ + z_at[dz], grp), False)

    listen(0, LAST - sum(far))
    send_rows(range(FIRST))
    send_ranks(False)
    listen(1, sum(far))
    send_ranks(True)
    send_rows(range(FIRST, LAST))
    R[LAST] = S[dp]
    Rr1[NZ - 1] = Sr[z]

    from_down, from_up, to_q2, to_d2 = {}, {}, {}, {}

    def span(t):
        lo, hi = SPANS[t]
        return lo, hi - lo, pl.ds(lo * MOST, (hi - lo) * MOST)

    def arrive(t):
        lo, places, at = span(t)
        wait_all(R.at[pl.ds(lo, places - (t == CHUNKS - 1))], row_r.at[t])
        count = places * MOST
        o0, o1 = iota((2 * count, 2 * count), 0), iota((2 * count, 2 * count), 1)
        whole = onehot(o1 == ((o0 % count) // MOST) * 8 + (o0 // count) * MOST + o0 % MOST).astype(BF16)
        rows = dot(whole, R[lo:lo + places].reshape(2 * count, half)).astype(BF16)
        K[0, lo * MOST:lo * MOST + count, :half] = rows[:count]
        K[0, lo * MOST:lo * MOST + count, half:] = rows[count:]
        from_down[t] = send(K.at[0, at], K.at[2, at], y_s.at[t, 0], y_r.at[t, 0], up)
        from_up[t] = send(K.at[0, at], K.at[1, at], y_s.at[t, 1], y_r.at[t, 1], down)
        to_q2[t] = send(K.at[0, at], Q2.at[at], y_s.at[t, 2], y_r.at[t, 2], sibling)

    def share(t):
        _, _, at = span(t)
        from_down[t].wait_recv()
        to_d2[t] = send(K.at[2, at], D2.at[at], y_s.at[t, 3], y_r.at[t, 3], sibling)

    arrive(0)
    arrive(1)

    wait_all(Rr1.at[pl.ds(0, NZ - 1)], rz_r)
    rx_copy = []
    for dx in range(1, NX):
        rx_copy.append(send(Rr1, Rr2.at[dx], rx_s.at[dx], rx_r.at[dx], (x_at[dx] + z, grp)))
    Rr2[0] = Rr1[...]
    share(0)
    share(1)
    arrive(2)
    for copy in rx_copy:
        copy.wait_recv()
    lanes = Rr2[...].reshape(GROUPS, 128)
    lane_high = jnp.floor(lanes * (1.0 / 256))
    lane_low = lanes - 256.0 * lane_high
    column = [dx * NZ + Z_ORDER.index(dz) for dx, dz in PLACES]
    r8, g1 = iota((8, GROUPS), 0), iota((8, GROUPS), 1)
    pick = jnp.concatenate(
        [onehot(g1 == jnp.where(r8 < MOST, column[p], column[p + 1])) for p in range(0, GROUPS, 2)], axis=0
    ).astype(BF16)
    both = dot(pick, jnp.concatenate([lane_high, lane_low], axis=1).astype(BF16))
    wide = both[:, :128] * 256.0 + both[:, 128:]
    w0, w1 = iota((SLOTS, 128), 0), iota((SLOTS, 128), 1)
    own_col = jnp.sum(jnp.where(w1 == x * MOST + w0 % MOST, wide, 0.0), axis=1, keepdims=True)
    d0, d1 = iota((SLOTS, SLOTS), 0), iota((SLOTS, SLOTS), 1)
    KR[0] = jnp.sum(jnp.where(d0 == d1, own_col, 0.0), axis=0, keepdims=True)
    yr_copy = [
        send(KR.at[0], KR.at[2], yr_s.at[0], yr_r.at[0], up),
        send(KR.at[0], KR.at[1], yr_s.at[1], yr_r.at[1], down),
        send(KR.at[0], QR2, yr_s.at[2], yr_r.at[2], sibling),
    ]

    arrive(3)
    rows8 = iota((8, 128), 0)
    cluster_of = []
    for p in range(0, GROUPS, 8):
        block = jnp.zeros((8, 128), jnp.int32)
        for i in range(8):
            block = jnp.where(rows8 == i, target[p + i], block)
        cluster_of.append(block)
    cluster_of = jnp.concatenate(cluster_of, axis=0).astype(F32)

    arrive(4)
    for copy in yr_copy:
        copy.wait_recv()
    dr_copy = send(KR.at[2], DR2, yr_s.at[3], yr_r.at[3], sibling)
    key_rank = [jnp.sum(jnp.where(d0 == d1, KR[b], 0.0), axis=1, keepdims=True) for b in range(3)]
    arrive(5)
    for t in range(2, CHUNKS):
        share(t)
    dr_copy.wait_recv()
    query_rank = [KR[0], QR2[...], KR[2], DR2[...]]
    query = [K.at[0], Q2, K.at[2], D2]

    def largest(c, chips):
        best = jnp.full((1, SLOTS), -1.0, F32)
        for b in chips:
            cosine = lax.dot_general(K[b], query[c][...], (((1,), (1,)), ((), ())), preferred_element_type=F32)
            masked = jnp.where(key_rank[b] < query_rank[c], cosine, -jnp.inf)
            best = jnp.maximum(best, jnp.max(masked, axis=0, keepdims=True))
        return best

    for t in range(CHUNKS):
        from_up[t].wait_recv()
        to_q2[t].wait_recv()
    PMs[0] = largest(1, range(3))
    pm_own = send(PMs.at[0], PM.at[0], pm_s.at[0], pm_r.at[0], sibling)
    own = largest(0, range(3))
    lower = largest(2, (1,))
    for t in range(CHUNKS):
        to_d2[t].wait_recv()
    PMs[1] = largest(3, (1,))
    pm_lower = send(PMs.at[1], PM.at[1], pm_s.at[1], pm_r.at[1], sibling)

    hops = [min(dx, NX - dx) + abs(dz) for dx, dz in PLACES]
    far_first = sorted(range(GROUPS), key=lambda p: -hops[p])

    def send_back(places):
        for p in places:
            if p < LAST:
                send(BS.at[p // 32], V.at[p], b_s.at[0], b_r.at[0], (source[p], grp), False)

    pm_own.wait_recv()
    own = jnp.maximum(own, PM[0])
    for i in range(2):
        BS[i] = own[:, i * 128:(i + 1) * 128]
    send_back(far_first[:24])
    pm_lower.wait_recv()
    lower = jnp.maximum(lower, PM[1])
    for i in range(2):
        BS[2 + i] = lower[:, i * 128:(i + 1) * 128]
    for p in far_first:
        send(BS.at[2 + p // 32], V.at[GROUPS + p], b_s.at[1], b_r.at[1], (source[p], below), False)
    send_back(far_first[24:])
    V[LAST] = BS[1]
    a0, a1 = iota((GROUPS, 128), 0), iota((GROUPS, 128), 1)
    first = (a0 % 32) * MOST
    hits = [(cluster_of == lab_row) & (slot_row == float(s)) for s in range(MOST)]
    mine = (a1 >= first) & (a1 < first + MOST)

    wait_all(R.at[pl.ds(0, LAST)], row_s)
    wait_all(Rr1.at[pl.ds(0, NZ - 1)], rz_s)
    wait_all(V.at[pl.ds(0, LAST)], b_s.at[0])
    wait_all(V.at[pl.ds(GROUPS, GROUPS)], b_s.at[1])
    for copy in started:
        copy.wait_send()

    wait_all(V.at[pl.ds(0, LAST)], b_r.at[0])
    wait_all(V.at[pl.ds(GROUPS, GROUPS)], b_r.at[1])
    back = jnp.maximum(V[:GROUPS], V[GROUPS:]).reshape(GROUPS, 128)
    held = jnp.where(mine, back, 0.0)
    shift = 64
    while shift >= MOST:
        held = held + pltpu.roll(held, shift, 1)
        shift //= 2
    chosen = jnp.zeros((GROUPS, 128), F32)
    for s in range(MOST):
        chosen = chosen + jnp.where(hits[s], held[:, s:s + 1], 0.0)
    out[...] = jnp.sum(chosen, axis=0, keepdims=True)


def body(embeddings, cluster, rank):
    rows, width = embeddings.shape
    sem = pltpu.SemaphoreType.DMA
    operands = [embeddings, cluster.reshape(1, rows), rank.reshape(1, rows)]
    operands = [pltpu.with_memory_space_constraint(operand, pltpu.HBM) for operand in operands]
    out = pl.pallas_call(
        kernel,
        out_shape=jax.ShapeDtypeStruct((1, rows), F32),
        in_specs=[pl.BlockSpec(memory_space=pltpu.HBM)] * 3,
        out_specs=pl.BlockSpec(memory_space=pltpu.VMEM),
        scratch_shapes=[
            pltpu.VMEM((rows, width), BF16),
            pltpu.VMEM((1, rows), jnp.int32),
            pltpu.VMEM((1, rows), jnp.int32),
            pltpu.VMEM((GROUPS, 8, width // 2), BF16),
            pltpu.VMEM((NZ, 1, 128), F32),
            pltpu.VMEM((GROUPS, 8, width // 2), BF16),
            pltpu.VMEM((NZ, 1, 128), F32),
            pltpu.VMEM((NX, NZ, 1, 128), F32),
            pltpu.VMEM((3, SLOTS, width), BF16),
            pltpu.VMEM((SLOTS, width), BF16),
            pltpu.VMEM((SLOTS, width), BF16),
            pltpu.VMEM((3, 1, SLOTS), F32),
            pltpu.VMEM((1, SLOTS), F32),
            pltpu.VMEM((1, SLOTS), F32),
            pltpu.VMEM((2, 1, SLOTS), F32),
            pltpu.VMEM((2, 1, SLOTS), F32),
            pltpu.VMEM((4, 1, 128), F32),
            pltpu.VMEM((2 * GROUPS, 1, 128), F32),
            pltpu.SemaphoreType.REGULAR,
            sem((3,)),
            sem, sem((CHUNKS,)), sem, sem, sem((NX,)), sem((NX,)),
            sem((CHUNKS, 4)), sem((CHUNKS, 4)), sem((4,)), sem((4,)),
            sem((2,)), sem((2,)), sem((2,)), sem((2,)),
        ],
        compiler_params=pltpu.CompilerParams(
            collective_id=0, has_side_effects=True, vmem_limit_bytes=40 * 1024 * 1024
        ),
    )(*operands)
    return out.reshape(rows)


def solution(mesh):
    in_specs = (P(("dp", "grp"), None), P(("dp", "grp"), None), P(("dp", "grp")))
    out_specs = P(("dp", "grp"))
    return jax.shard_map(body, mesh=mesh, in_specs=in_specs, out_specs=out_specs, check_vma=False)
```

```python
import jax
import jax.numpy as jnp
from jax import lax
from jax.experimental import pallas as pl
from jax.experimental.pallas import tpu as pltpu
from jax.sharding import PartitionSpec as P

NX, NY, NZ = 4, 4, 16
GROUPS = NX * NZ
MOST = 4
SLOTS = GROUPS * MOST
EMPTY = 65536.0

REACH = 4
DZ_NEAR = [4, -4, 3, -3, 2, -2, 1, -1, 0]
DZ_FAR = [8, -7, 7, -6, 6, -5, 5]
NEAR = [(dx, dz) for dx in (2, 1, 3, 0) for dz in DZ_NEAR][:-1]
PLACES = NEAR + [(dx, dz) for dx in (2, 1, 3, 0) for dz in DZ_FAR] + [(0, 0)]
FIRST = len(NEAR)
SPANS = [(0, 16), (16, 32), (32, 40), (40, 48), (48, 56), (56, 64)]
CHUNKS = len(SPANS)
Z_ORDER = [8, -7, 7, -6, 6, -5, 5, -4, 4, -3, 3, -2, 2, -1, 1, 0]
LAST = GROUPS - 1
WINDOWS = [(0, FIRST), (FIRST, 40), (40, 48), (48, 56), (56, LAST)]

F32, BF16 = jnp.float32, jnp.bfloat16


def iota(shape, dim):
    return lax.broadcasted_iota(jnp.int32, shape, dim)


def onehot(cond):
    return jnp.where(cond, 1.0, 0.0)


def dot(a, b):
    return lax.dot_general(a, b, (((1,), (0,)), ((), ())), preferred_element_type=F32)


def kernel(emb_in, lab_in, rank_in, out, emb, lab, rank, S, Sr, R, Rr1, Rr2, K, Q2, D2, KR, QR2, DR2, PM, PMs, BS, V,
           gate, in_s, row_s, row_r, rz_s, rz_r, rx_s, rx_r, y_s, y_r, yr_s, yr_r, pm_s, pm_r, b_s, b_r):
    dp, grp = lax.axis_index("dp"), lax.axis_index("grp")
    x, z = lax.div(dp, NZ), lax.rem(dp, NZ)
    y, core = lax.div(grp, 2), lax.rem(grp, 2)
    z_at = {dz: lax.rem(z + (dz + NZ), NZ) for dz in range(1 - NZ // 2, NZ // 2 + 1)}
    z_from = {dz: lax.rem(z + (NZ - dz), NZ) for dz in z_at}
    x_at = [lax.rem(x + dx, NX) * NZ for dx in range(NX)]
    x_from = [lax.rem(x + (NX - dx), NX) * NZ for dx in range(NX)]
    target = [x_at[dx] + z_at[dz] for dx, dz in PLACES]
    source = [x_from[dx] + z_from[dz] for dx, dz in PLACES]

    up = (dp, lax.rem(y + 1, NY) * 2 + core)
    below = lax.rem(y + (NY - 1), NY) * 2 + core
    down = (dp, below)
    sibling = (dp, y * 2 + 1 - core)
    mesh_id = pl.DeviceIdType.MESH
    started = []

    def send(src, dst, send_sem, recv_sem, to, keep=True):
        copy = pltpu.make_async_remote_copy(
            src_ref=src, dst_ref=dst, send_sem=send_sem, recv_sem=recv_sem, device_id=to, device_id_type=mesh_id
        )
        copy.start()
        if keep:
            started.append(copy)
        return copy

    def wait_all(ref, sem):
        pltpu.make_async_copy(ref, ref, sem).wait()

    barrier = pltpu.get_barrier_semaphore()
    far = [abs(dz) > REACH for _, dz in PLACES]
    peers = [(target[p], y * 2 + int(far[p])) for p in range(LAST)] + [up, down, sibling]
    distance = [min(dx, NX - dx) + abs(dz) for dx, dz in PLACES]
    peers[:LAST] = [peers[p] for p in sorted(range(LAST), key=lambda p: -distance[p])]
    for peer in peers:
        pl.semaphore_signal(barrier, inc=1, device_id=peer, device_id_type=mesh_id)

    def listen(reach, count):
        @pl.when(core == reach)
        def _():
            pl.semaphore_wait(barrier, 2 * count + 3)
            pl.semaphore_signal(gate, inc=1, device_id=sibling, device_id_type=mesh_id)

        @pl.when(core != reach)
        def _():
            pl.semaphore_wait(gate, 1)

    loads = [pltpu.make_async_copy(a, b, in_s.at[i]) for i, (a, b) in enumerate(
        ((lab_in, lab), (rank_in, rank), (emb_in, emb)))]
    for load in loads:
        load.start()
    loads[0].wait()
    loads[1].wait()

    lab_row = lab[...].astype(F32)
    i0, i1 = iota((128, 128), 0), iota((128, 128), 1)
    lab_all = jnp.broadcast_to(lab_row, (128, 128))
    lab_col = jnp.sum(jnp.where(i0 == i1, lab_all, 0.0), axis=1, keepdims=True)
    same = onehot(lab_col == lab_all)
    slot_row = jnp.sum(jnp.where(i0 < i1, same, 0.0), axis=0, keepdims=True)
    slot_col = jnp.sum(jnp.where(i1 < i0, same, 0.0), axis=1, keepdims=True)
    pos_row = lab_row * MOST + slot_row

    rank_row = rank[...].astype(F32)
    high = jnp.floor(rank_row * (1.0 / 256))
    low = rank_row - 256.0 * high
    xg_row = jnp.floor(lab_row * (1.0 / NZ))
    xg_col = jnp.floor(lab_col * (1.0 / NZ))
    mine = lab_row - NZ * xg_row == iota((NZ, 128), 0).astype(F32)
    parts = jnp.concatenate(
        [jnp.where(mine, high, 0.0), jnp.where(mine, low, 0.0), onehot(mine)], axis=0
    ).astype(BF16)
    place = onehot(xg_col * MOST + slot_col == i1.astype(F32)).astype(BF16)
    found = dot(parts, place)
    ranks = found[:NZ] * 256.0 + found[NZ:2 * NZ] + (1.0 - found[2 * NZ:]) * EMPTY
    for i in range(NZ):
        Sr[i] = ranks[i:i + 1]

    width = emb.shape[1]
    half = width // 2
    s0, s1 = iota((2 * SLOTS, 256), 0), iota((2 * SLOTS, 256), 1)
    slot_of = (s0 // 8) * MOST + s0 % MOST
    pos_two = jnp.concatenate([pos_row, pos_row], axis=1)
    spread = onehot((pos_two == slot_of.astype(F32)) & ((s0 // MOST) % 2 == s1 // 128)).astype(BF16)
    loads[2].wait()
    values = emb[...].astype(F32)
    scale = lax.rsqrt(jnp.mean(values * values, axis=1, keepdims=True) + 1e-06) / jnp.sqrt(F32(width))
    unit = (values * scale).astype(BF16)
    S[...] = dot(spread, jnp.concatenate([unit[:, :half], unit[:, half:]], axis=0)).astype(BF16).reshape(S.shape)

    chunk_of = [t for t, (lo, hi) in enumerate(SPANS) for _ in range(lo, hi)]

    window_of = [w for w, (lo, hi) in enumerate(WINDOWS) for _ in range(lo, hi)]

    def sent(w):
        lo, hi = WINDOWS[w]
        wait_all(R.at[pl.ds(lo, hi - lo)], row_s.at[w])

    def send_rows(places):
        for p in places:
            send(S.at[target[p]], R.at[p], row_s.at[window_of[p]], row_r.at[chunk_of[p]], (target[p], grp), False)

    def send_ranks(distant):
        for i, dz in enumerate(Z_ORDER[:NZ - 1]):
            if (abs(dz) > REACH) == distant:
                send(Sr.at[z_at[dz]], Rr1.at[i], rz_s, rz_r, (x * NZ + z_at[dz], grp), False)

    listen(0, LAST - sum(far))
    send_rows(range(FIRST))
    send_ranks(False)
    listen(1, sum(far))
    send_ranks(True)
    send_rows(range(FIRST, 48))
    R[LAST] = S[dp]
    Rr1[NZ - 1] = Sr[z]

    from_down, from_up, to_q2, to_d2 = {}, {}, {}, {}

    def span(t):
        lo, hi = SPANS[t]
        return lo, hi - lo, pl.ds(lo * MOST, (hi - lo) * MOST)

    def arrive(t):
        lo, places, at = span(t)
        wait_all(R.at[pl.ds(lo, places - (t == CHUNKS - 1))], row_r.at[t])
        count = places * MOST
        o0, o1 = iota((2 * count, 2 * count), 0), iota((2 * count, 2 * count), 1)
        whole = onehot(o1 == ((o0 % count) // MOST) * 8 + (o0 // count) * MOST + o0 % MOST).astype(BF16)
        rows = dot(whole, R[lo:lo + places].reshape(2 * count, half)).astype(BF16)
        K[0, lo * MOST:lo * MOST + count, :half] = rows[:count]
        K[0, lo * MOST:lo * MOST + count, half:] = rows[count:]
        from_down[t] = send(K.at[0, at], K.at[2, at], y_s.at[t, 0], y_r.at[t, 0], up)
        from_up[t] = send(K.at[0, at], K.at[1, at], y_s.at[t, 1], y_r.at[t, 1], down)
        to_q2[t] = send(K.at[0, at], Q2.at[at], y_s.at[t, 2], y_r.at[t, 2], sibling)

    def share(t):
        _, _, at = span(t)
        from_down[t].wait_recv()
        to_d2[t] = send(K.at[2, at], D2.at[at], y_s.at[t, 3], y_r.at[t, 3], sibling)

    arrive(0)
    sent(1)
    send_rows(range(48, 56))
    arrive(1)
    sent(2)
    send_rows(range(56, LAST))

    wait_all(Rr1.at[pl.ds(0, NZ - 1)], rz_r)
    rx_copy = []
    for dx in range(1, NX):
        rx_copy.append(send(Rr1, Rr2.at[dx], rx_s.at[dx], rx_r.at[dx], (x_at[dx] + z, grp)))
    Rr2[0] = Rr1[...]
    share(0)
    share(1)
    arrive(2)
    for copy in rx_copy:
        copy.wait_recv()
    lanes = Rr2[...].reshape(GROUPS, 128)
    lane_high = jnp.floor(lanes * (1.0 / 256))
    lane_low = lanes - 256.0 * lane_high
    column = [dx * NZ + Z_ORDER.index(dz) for dx, dz in PLACES]
    r8, g1 = iota((8, GROUPS), 0), iota((8, GROUPS), 1)
    pick = jnp.concatenate(
        [onehot(g1 == jnp.where(r8 < MOST, column[p], column[p + 1])) for p in range(0, GROUPS, 2)], axis=0
    ).astype(BF16)
    both = dot(pick, jnp.concatenate([lane_high, lane_low], axis=1).astype(BF16))
    wide = both[:, :128] * 256.0 + both[:, 128:]
    w0, w1 = iota((SLOTS, 128), 0), iota((SLOTS, 128), 1)
    own_col = jnp.sum(jnp.where(w1 == x * MOST + w0 % MOST, wide, 0.0), axis=1, keepdims=True)
    d0, d1 = iota((SLOTS, SLOTS), 0), iota((SLOTS, SLOTS), 1)
    KR[0] = jnp.sum(jnp.where(d0 == d1, own_col, 0.0), axis=0, keepdims=True)
    yr_copy = [
        send(KR.at[0], KR.at[2], yr_s.at[0], yr_r.at[0], up),
        send(KR.at[0], KR.at[1], yr_s.at[1], yr_r.at[1], down),
        send(KR.at[0], QR2, yr_s.at[2], yr_r.at[2], sibling),
    ]

    arrive(3)
    rows8 = iota((8, 128), 0)
    cluster_of = []
    for p in range(0, GROUPS, 8):
        block = jnp.zeros((8, 128), jnp.int32)
        for i in range(8):
            block = jnp.where(rows8 == i, target[p + i], block)
        cluster_of.append(block)
    cluster_of = jnp.concatenate(cluster_of, axis=0).astype(F32)

    arrive(4)
    for copy in yr_copy:
        copy.wait_recv()
    dr_copy = send(KR.at[2], DR2, yr_s.at[3], yr_r.at[3], sibling)
    key_rank = [jnp.sum(jnp.where(d0 == d1, KR[b], 0.0), axis=1, keepdims=True) for b in range(3)]
    arrive(5)
    for t in range(2, CHUNKS):
        share(t)
    dr_copy.wait_recv()
    query_rank = [KR[0], QR2[...], KR[2], DR2[...]]
    query = [K.at[0], Q2, K.at[2], D2]

    def largest(c, chips):
        best = jnp.full((1, SLOTS), -1.0, F32)
        for b in chips:
            cosine = lax.dot_general(K[b], query[c][...], (((1,), (1,)), ((), ())), preferred_element_type=F32)
            masked = jnp.where(key_rank[b] < query_rank[c], cosine, -jnp.inf)
            best = jnp.maximum(best, jnp.max(masked, axis=0, keepdims=True))
        return best

    for t in range(CHUNKS):
        from_up[t].wait_recv()
        to_q2[t].wait_recv()
    PMs[0] = largest(1, range(3))
    pm_own = send(PMs.at[0], PM.at[0], pm_s.at[0], pm_r.at[0], sibling)
    own = largest(0, range(3))
    lower = largest(2, (1,))
    for t in range(CHUNKS):
        to_d2[t].wait_recv()
    PMs[1] = largest(3, (1,))
    pm_lower = send(PMs.at[1], PM.at[1], pm_s.at[1], pm_r.at[1], sibling)

    hops = [min(dx, NX - dx) + abs(dz) for dx, dz in PLACES]
    far_first = sorted(range(GROUPS), key=lambda p: -hops[p])

    def send_back(places):
        for p in places:
            if p < LAST:
                send(BS.at[p // 32], V.at[p], b_s.at[0], b_r.at[0], (source[p], grp), False)

    pm_own.wait_recv()
    own = jnp.maximum(own, PM[0])
    for i in range(2):
        BS[i] = own[:, i * 128:(i + 1) * 128]
    send_back(far_first[:24])
    pm_lower.wait_recv()
    lower = jnp.maximum(lower, PM[1])
    for i in range(2):
        BS[2 + i] = lower[:, i * 128:(i + 1) * 128]
    for p in far_first:
        send(BS.at[2 + p // 32], V.at[GROUPS + p], b_s.at[1], b_r.at[1], (source[p], below), False)
    send_back(far_first[24:])
    V[LAST] = BS[1]
    a0, a1 = iota((GROUPS, 128), 0), iota((GROUPS, 128), 1)
    first = (a0 % 32) * MOST
    hits = [(cluster_of == lab_row) & (slot_row == float(s)) for s in range(MOST)]
    mine = (a1 >= first) & (a1 < first + MOST)

    for w in (0, 3, 4):
        sent(w)
    wait_all(Rr1.at[pl.ds(0, NZ - 1)], rz_s)
    wait_all(V.at[pl.ds(0, LAST)], b_s.at[0])
    wait_all(V.at[pl.ds(GROUPS, GROUPS)], b_s.at[1])
    for copy in started:
        copy.wait_send()

    wait_all(V.at[pl.ds(0, LAST)], b_r.at[0])
    wait_all(V.at[pl.ds(GROUPS, GROUPS)], b_r.at[1])
    back = jnp.maximum(V[:GROUPS], V[GROUPS:]).reshape(GROUPS, 128)
    held = jnp.where(mine, back, 0.0)
    shift = 64
    while shift >= MOST:
        held = held + pltpu.roll(held, shift, 1)
        shift //= 2
    chosen = jnp.zeros((GROUPS, 128), F32)
    for s in range(MOST):
        chosen = chosen + jnp.where(hits[s], held[:, s:s + 1], 0.0)
    out[...] = jnp.sum(chosen, axis=0, keepdims=True)


def body(embeddings, cluster, rank):
    rows, width = embeddings.shape
    sem = pltpu.SemaphoreType.DMA
    operands = [embeddings, cluster.reshape(1, rows), rank.reshape(1, rows)]
    operands = [pltpu.with_memory_space_constraint(operand, pltpu.HBM) for operand in operands]
    out = pl.pallas_call(
        kernel,
        out_shape=jax.ShapeDtypeStruct((1, rows), F32),
        in_specs=[pl.BlockSpec(memory_space=pltpu.HBM)] * 3,
        out_specs=pl.BlockSpec(memory_space=pltpu.VMEM),
        scratch_shapes=[
            pltpu.VMEM((rows, width), BF16),
            pltpu.VMEM((1, rows), jnp.int32),
            pltpu.VMEM((1, rows), jnp.int32),
            pltpu.VMEM((GROUPS, 8, width // 2), BF16),
            pltpu.VMEM((NZ, 1, 128), F32),
            pltpu.VMEM((GROUPS, 8, width // 2), BF16),
            pltpu.VMEM((NZ, 1, 128), F32),
            pltpu.VMEM((NX, NZ, 1, 128), F32),
            pltpu.VMEM((3, SLOTS, width), BF16),
            pltpu.VMEM((SLOTS, width), BF16),
            pltpu.VMEM((SLOTS, width), BF16),
            pltpu.VMEM((3, 1, SLOTS), F32),
            pltpu.VMEM((1, SLOTS), F32),
            pltpu.VMEM((1, SLOTS), F32),
            pltpu.VMEM((2, 1, SLOTS), F32),
            pltpu.VMEM((2, 1, SLOTS), F32),
            pltpu.VMEM((4, 1, 128), F32),
            pltpu.VMEM((2 * GROUPS, 1, 128), F32),
            pltpu.SemaphoreType.REGULAR,
            sem((3,)),
            sem((len(WINDOWS),)), sem((CHUNKS,)), sem, sem, sem((NX,)), sem((NX,)),
            sem((CHUNKS, 4)), sem((CHUNKS, 4)), sem((4,)), sem((4,)),
            sem((2,)), sem((2,)), sem((2,)), sem((2,)),
        ],
        compiler_params=pltpu.CompilerParams(
            collective_id=0, has_side_effects=True, vmem_limit_bytes=40 * 1024 * 1024
        ),
    )(*operands)
    return out.reshape(rows)


def solution(mesh):
    in_specs = (P(("dp", "grp"), None), P(("dp", "grp"), None), P(("dp", "grp")))
    out_specs = P(("dp", "grp"))
    return jax.shard_map(body, mesh=mesh, in_specs=in_specs, out_specs=out_specs, check_vma=False)
```

```python
import jax
import jax.numpy as jnp
from jax import lax
from jax.experimental import pallas as pl
from jax.experimental.pallas import tpu as pltpu
from jax.sharding import PartitionSpec as P

NX, NY, NZ = 4, 4, 16
GROUPS = NX * NZ
MOST = 4
SLOTS = GROUPS * MOST
EMPTY = 65536.0

REACH = 4
DZ_NEAR = [4, -4, 3, -3, 2, -2, 1, -1, 0]
DZ_FAR = [8, -7, 7, -6, 6, -5, 5]
NEAR = [(dx, dz) for dx in (2, 1, 3, 0) for dz in DZ_NEAR][:-1]
PLACES = NEAR + [(dx, dz) for dx in (2, 1, 3, 0) for dz in DZ_FAR] + [(0, 0)]
FIRST = len(NEAR)
SPANS = [(0, 16), (16, 32), (32, 40), (40, 48), (48, 56), (56, 60), (60, 64)]
CHUNKS = len(SPANS)
Z_ORDER = [8, -7, 7, -6, 6, -5, 5, -4, 4, -3, 3, -2, 2, -1, 1, 0]
LAST = GROUPS - 1

F32, BF16 = jnp.float32, jnp.bfloat16


def iota(shape, dim):
    return lax.broadcasted_iota(jnp.int32, shape, dim)


def onehot(cond):
    return jnp.where(cond, 1.0, 0.0)


def dot(a, b):
    return lax.dot_general(a, b, (((1,), (0,)), ((), ())), preferred_element_type=F32)


def kernel(emb_in, lab_in, rank_in, out, emb, lab, rank, S, Sr, R, Rr1, Rr2, K, Q2, D2, KR, QR2, DR2, PM, PMs, BS, V,
           gate, in_s, row_s, row_r, rz_s, rz_r, rx_s, rx_r, y_s, y_r, yr_s, yr_r, pm_s, pm_r, b_s, b_r):
    dp, grp = lax.axis_index("dp"), lax.axis_index("grp")
    x, z = lax.div(dp, NZ), lax.rem(dp, NZ)
    y, core = lax.div(grp, 2), lax.rem(grp, 2)
    z_at = {dz: lax.rem(z + (dz + NZ), NZ) for dz in range(1 - NZ // 2, NZ // 2 + 1)}
    z_from = {dz: lax.rem(z + (NZ - dz), NZ) for dz in z_at}
    x_at = [lax.rem(x + dx, NX) * NZ for dx in range(NX)]
    x_from = [lax.rem(x + (NX - dx), NX) * NZ for dx in range(NX)]
    target = [x_at[dx] + z_at[dz] for dx, dz in PLACES]
    source = [x_from[dx] + z_from[dz] for dx, dz in PLACES]

    up = (dp, lax.rem(y + 1, NY) * 2 + core)
    below = lax.rem(y + (NY - 1), NY) * 2 + core
    down = (dp, below)
    sibling = (dp, y * 2 + 1 - core)
    mesh_id = pl.DeviceIdType.MESH
    started = []

    def send(src, dst, send_sem, recv_sem, to, keep=True):
        copy = pltpu.make_async_remote_copy(
            src_ref=src, dst_ref=dst, send_sem=send_sem, recv_sem=recv_sem, device_id=to, device_id_type=mesh_id
        )
        copy.start()
        if keep:
            started.append(copy)
        return copy

    def wait_all(ref, sem):
        pltpu.make_async_copy(ref, ref, sem).wait()

    barrier = pltpu.get_barrier_semaphore()
    far = [abs(dz) > REACH for _, dz in PLACES]
    peers = [(target[p], y * 2 + int(far[p])) for p in range(LAST)] + [up, down, sibling]
    distance = [min(dx, NX - dx) + abs(dz) for dx, dz in PLACES]
    peers[:LAST] = [peers[p] for p in sorted(range(LAST), key=lambda p: -distance[p])]
    for peer in peers:
        pl.semaphore_signal(barrier, inc=1, device_id=peer, device_id_type=mesh_id)

    def listen(reach, count):
        @pl.when(core == reach)
        def _():
            pl.semaphore_wait(barrier, 2 * count + 3)
            pl.semaphore_signal(gate, inc=1, device_id=sibling, device_id_type=mesh_id)

        @pl.when(core != reach)
        def _():
            pl.semaphore_wait(gate, 1)

    loads = [pltpu.make_async_copy(a, b, in_s.at[i]) for i, (a, b) in enumerate(
        ((lab_in, lab), (rank_in, rank), (emb_in, emb)))]
    for load in loads:
        load.start()
    loads[0].wait()
    loads[1].wait()

    lab_row = lab[...].astype(F32)
    i0, i1 = iota((128, 128), 0), iota((128, 128), 1)
    lab_all = jnp.broadcast_to(lab_row, (128, 128))
    lab_col = jnp.sum(jnp.where(i0 == i1, lab_all, 0.0), axis=1, keepdims=True)
    same = onehot(lab_col == lab_all)
    slot_row = jnp.sum(jnp.where(i0 < i1, same, 0.0), axis=0, keepdims=True)
    slot_col = jnp.sum(jnp.where(i1 < i0, same, 0.0), axis=1, keepdims=True)
    pos_row = lab_row * MOST + slot_row

    rank_row = rank[...].astype(F32)
    high = jnp.floor(rank_row * (1.0 / 256))
    low = rank_row - 256.0 * high
    xg_row = jnp.floor(lab_row * (1.0 / NZ))
    xg_col = jnp.floor(lab_col * (1.0 / NZ))
    mine = lab_row - NZ * xg_row == iota((NZ, 128), 0).astype(F32)
    parts = jnp.concatenate(
        [jnp.where(mine, high, 0.0), jnp.where(mine, low, 0.0), onehot(mine)], axis=0
    ).astype(BF16)
    place = onehot(xg_col * MOST + slot_col == i1.astype(F32)).astype(BF16)
    found = dot(parts, place)
    ranks = found[:NZ] * 256.0 + found[NZ:2 * NZ] + (1.0 - found[2 * NZ:]) * EMPTY
    for i in range(NZ):
        Sr[i] = ranks[i:i + 1]

    width = emb.shape[1]
    half = width // 2
    s0, s1 = iota((2 * SLOTS, 256), 0), iota((2 * SLOTS, 256), 1)
    slot_of = (s0 // 8) * MOST + s0 % MOST
    pos_two = jnp.concatenate([pos_row, pos_row], axis=1)
    spread = onehot((pos_two == slot_of.astype(F32)) & ((s0 // MOST) % 2 == s1 // 128)).astype(BF16)
    loads[2].wait()
    values = emb[...].astype(F32)
    scale = lax.rsqrt(jnp.mean(values * values, axis=1, keepdims=True) + 1e-06) / jnp.sqrt(F32(width))
    unit = (values * scale).astype(BF16)
    S[...] = dot(spread, jnp.concatenate([unit[:, :half], unit[:, half:]], axis=0)).astype(BF16).reshape(S.shape)

    chunk_of = [t for t, (lo, hi) in enumerate(SPANS) for _ in range(lo, hi)]

    def send_rows(places):
        for p in places:
            send(S.at[target[p]], R.at[p], row_s, row_r.at[chunk_of[p]], (target[p], grp), False)

    def send_ranks(distant):
        for i, dz in enumerate(Z_ORDER[:NZ - 1]):
            if (abs(dz) > REACH) == distant:
                send(Sr.at[z_at[dz]], Rr1.at[i], rz_s, rz_r, (x * NZ + z_at[dz], grp), False)

    listen(0, LAST - sum(far))
    send_rows(range(FIRST))
    send_ranks(False)
    listen(1, sum(far))
    send_ranks(True)
    send_rows(range(FIRST, LAST))
    R[LAST] = S[dp]
    Rr1[NZ - 1] = Sr[z]

    from_down, from_up, to_q2, to_d2 = {}, {}, {}, {}

    def span(t):
        lo, hi = SPANS[t]
        return lo, hi - lo, pl.ds(lo * MOST, (hi - lo) * MOST)

    def arrive(t):
        lo, places, at = span(t)
        wait_all(R.at[pl.ds(lo, places - (t == CHUNKS - 1))], row_r.at[t])
        count = places * MOST
        o0, o1 = iota((2 * count, 2 * count), 0), iota((2 * count, 2 * count), 1)
        whole = onehot(o1 == ((o0 % count) // MOST) * 8 + (o0 // count) * MOST + o0 % MOST).astype(BF16)
        rows = dot(whole, R[lo:lo + places].reshape(2 * count, half)).astype(BF16)
        K[0, lo * MOST:lo * MOST + count, :half] = rows[:count]
        K[0, lo * MOST:lo * MOST + count, half:] = rows[count:]
        from_down[t] = send(K.at[0, at], K.at[2, at], y_s.at[t, 0], y_r.at[t, 0], up)
        from_up[t] = send(K.at[0, at], K.at[1, at], y_s.at[t, 1], y_r.at[t, 1], down)
        to_q2[t] = send(K.at[0, at], Q2.at[at], y_s.at[t, 2], y_r.at[t, 2], sibling)

    def share(t):
        _, _, at = span(t)
        from_down[t].wait_recv()
        to_d2[t] = send(K.at[2, at], D2.at[at], y_s.at[t, 3], y_r.at[t, 3], sibling)

    arrive(0)
    arrive(1)

    wait_all(Rr1.at[pl.ds(0, NZ - 1)], rz_r)
    rx_copy = []
    for dx in range(1, NX):
        rx_copy.append(send(Rr1, Rr2.at[dx], rx_s.at[dx], rx_r.at[dx], (x_at[dx] + z, grp)))
    Rr2[0] = Rr1[...]
    share(0)
    share(1)
    arrive(2)
    for copy in rx_copy:
        copy.wait_recv()
    lanes = Rr2[...].reshape(GROUPS, 128)
    lane_high = jnp.floor(lanes * (1.0 / 256))
    lane_low = lanes - 256.0 * lane_high
    column = [dx * NZ + Z_ORDER.index(dz) for dx, dz in PLACES]
    r8, g1 = iota((8, GROUPS), 0), iota((8, GROUPS), 1)
    pick = jnp.concatenate(
        [onehot(g1 == jnp.where(r8 < MOST, column[p], column[p + 1])) for p in range(0, GROUPS, 2)], axis=0
    ).astype(BF16)
    both = dot(pick, jnp.concatenate([lane_high, lane_low], axis=1).astype(BF16))
    wide = both[:, :128] * 256.0 + both[:, 128:]
    w0, w1 = iota((SLOTS, 128), 0), iota((SLOTS, 128), 1)
    own_col = jnp.sum(jnp.where(w1 == x * MOST + w0 % MOST, wide, 0.0), axis=1, keepdims=True)
    d0, d1 = iota((SLOTS, SLOTS), 0), iota((SLOTS, SLOTS), 1)
    KR[0] = jnp.sum(jnp.where(d0 == d1, own_col, 0.0), axis=0, keepdims=True)
    yr_copy = [
        send(KR.at[0], KR.at[2], yr_s.at[0], yr_r.at[0], up),
        send(KR.at[0], KR.at[1], yr_s.at[1], yr_r.at[1], down),
        send(KR.at[0], QR2, yr_s.at[2], yr_r.at[2], sibling),
    ]

    arrive(3)
    rows8 = iota((8, 128), 0)
    cluster_of = []
    for p in range(0, GROUPS, 8):
        block = jnp.zeros((8, 128), jnp.int32)
        for i in range(8):
            block = jnp.where(rows8 == i, target[p + i], block)
        cluster_of.append(block)
    cluster_of = jnp.concatenate(cluster_of, axis=0).astype(F32)

    arrive(4)
    for copy in yr_copy:
        copy.wait_recv()
    dr_copy = send(KR.at[2], DR2, yr_s.at[3], yr_r.at[3], sibling)
    key_rank = [jnp.sum(jnp.where(d0 == d1, KR[b], 0.0), axis=1, keepdims=True) for b in range(3)]
    arrive(5)
    arrive(6)
    for t in range(2, CHUNKS):
        share(t)
    dr_copy.wait_recv()
    query_rank = [KR[0], QR2[...], KR[2], DR2[...]]
    query = [K.at[0], Q2, K.at[2], D2]

    def largest(c, chips):
        best = jnp.full((1, SLOTS), -1.0, F32)
        for b in chips:
            cosine = lax.dot_general(K[b], query[c][...], (((1,), (1,)), ((), ())), preferred_element_type=F32)
            masked = jnp.where(key_rank[b] < query_rank[c], cosine, -jnp.inf)
            best = jnp.maximum(best, jnp.max(masked, axis=0, keepdims=True))
        return best

    for t in range(CHUNKS):
        from_up[t].wait_recv()
        to_q2[t].wait_recv()
    PMs[0] = largest(1, range(3))
    pm_own = send(PMs.at[0], PM.at[0], pm_s.at[0], pm_r.at[0], sibling)
    own = largest(0, range(3))
    lower = largest(2, (1,))
    for t in range(CHUNKS):
        to_d2[t].wait_recv()
    PMs[1] = largest(3, (1,))
    pm_lower = send(PMs.at[1], PM.at[1], pm_s.at[1], pm_r.at[1], sibling)

    hops = [min(dx, NX - dx) + abs(dz) for dx, dz in PLACES]
    far_first = sorted(range(GROUPS), key=lambda p: -hops[p])

    def send_back(places):
        for p in places:
            if p < LAST:
                send(BS.at[p // 32], V.at[p], b_s.at[0], b_r.at[0], (source[p], grp), False)

    pm_own.wait_recv()
    own = jnp.maximum(own, PM[0])
    for i in range(2):
        BS[i] = own[:, i * 128:(i + 1) * 128]
    send_back(far_first[:24])
    pm_lower.wait_recv()
    lower = jnp.maximum(lower, PM[1])
    for i in range(2):
        BS[2 + i] = lower[:, i * 128:(i + 1) * 128]
    for p in far_first:
        send(BS.at[2 + p // 32], V.at[GROUPS + p], b_s.at[1], b_r.at[1], (source[p], below), False)
    send_back(far_first[24:])
    V[LAST] = BS[1]
    a0, a1 = iota((GROUPS, 128), 0), iota((GROUPS, 128), 1)
    first = (a0 % 32) * MOST
    hits = [(cluster_of == lab_row) & (slot_row == float(s)) for s in range(MOST)]
    mine = (a1 >= first) & (a1 < first + MOST)

    wait_all(R.at[pl.ds(0, LAST)], row_s)
    wait_all(Rr1.at[pl.ds(0, NZ - 1)], rz_s)
    wait_all(V.at[pl.ds(0, LAST)], b_s.at[0])
    wait_all(V.at[pl.ds(GROUPS, GROUPS)], b_s.at[1])
    for copy in started:
        copy.wait_send()

    wait_all(V.at[pl.ds(0, LAST)], b_r.at[0])
    wait_all(V.at[pl.ds(GROUPS, GROUPS)], b_r.at[1])
    back = jnp.maximum(V[:GROUPS], V[GROUPS:]).reshape(GROUPS, 128)
    held = jnp.where(mine, back, 0.0)
    shift = 64
    while shift >= MOST:
        held = held + pltpu.roll(held, shift, 1)
        shift //= 2
    chosen = jnp.zeros((GROUPS, 128), F32)
    for s in range(MOST):
        chosen = chosen + jnp.where(hits[s], held[:, s:s + 1], 0.0)
    out[...] = jnp.sum(chosen, axis=0, keepdims=True)


def body(embeddings, cluster, rank):
    rows, width = embeddings.shape
    sem = pltpu.SemaphoreType.DMA
    operands = [embeddings, cluster.reshape(1, rows), rank.reshape(1, rows)]
    operands = [pltpu.with_memory_space_constraint(operand, pltpu.HBM) for operand in operands]
    out = pl.pallas_call(
        kernel,
        out_shape=jax.ShapeDtypeStruct((1, rows), F32),
        in_specs=[pl.BlockSpec(memory_space=pltpu.HBM)] * 3,
        out_specs=pl.BlockSpec(memory_space=pltpu.VMEM),
        scratch_shapes=[
            pltpu.VMEM((rows, width), BF16),
            pltpu.VMEM((1, rows), jnp.int32),
            pltpu.VMEM((1, rows), jnp.int32),
            pltpu.VMEM((GROUPS, 8, width // 2), BF16),
            pltpu.VMEM((NZ, 1, 128), F32),
            pltpu.VMEM((GROUPS, 8, width // 2), BF16),
            pltpu.VMEM((NZ, 1, 128), F32),
            pltpu.VMEM((NX, NZ, 1, 128), F32),
            pltpu.VMEM((3, SLOTS, width), BF16),
            pltpu.VMEM((SLOTS, width), BF16),
            pltpu.VMEM((SLOTS, width), BF16),
            pltpu.VMEM((3, 1, SLOTS), F32),
            pltpu.VMEM((1, SLOTS), F32),
            pltpu.VMEM((1, SLOTS), F32),
            pltpu.VMEM((2, 1, SLOTS), F32),
            pltpu.VMEM((2, 1, SLOTS), F32),
            pltpu.VMEM((4, 1, 128), F32),
            pltpu.VMEM((2 * GROUPS, 1, 128), F32),
            pltpu.SemaphoreType.REGULAR,
            sem((3,)),
            sem, sem((CHUNKS,)), sem, sem, sem((NX,)), sem((NX,)),
            sem((CHUNKS, 4)), sem((CHUNKS, 4)), sem((4,)), sem((4,)),
            sem((2,)), sem((2,)), sem((2,)), sem((2,)),
        ],
        compiler_params=pltpu.CompilerParams(
            collective_id=0, has_side_effects=True, vmem_limit_bytes=40 * 1024 * 1024
        ),
    )(*operands)
    return out.reshape(rows)


def solution(mesh):
    in_specs = (P(("dp", "grp"), None), P(("dp", "grp"), None), P(("dp", "grp")))
    out_specs = P(("dp", "grp"))
    return jax.shard_map(body, mesh=mesh, in_specs=in_specs, out_specs=out_specs, check_vma=False)
```
